32 devices in a mesh: gx: 2 (over y), gy: 8 (over z, core), gz: 2 (over x).
Axes of the slice: x: 2, y: 2, z: 4, core: 2. Of those that a mesh axis runs over, the one named last changes fastest.
Arguments:
- flow_vector_lowres: float32 [3, 4, 256, 256], P(None, 'gz', 'gy', 'gx'), may hold values from -3 to 3
- heat_anomaly_lowres: float32 [4, 256, 256], P('gz', 'gy', 'gx'), may hold values from -6 to 6
- salt_content_anomaly: float32 [8, 512, 512], P('gz', ('gx', 'gy')), may hold values from -6 to 6
Outputs:
- updated_velocity: float32 [3, 4, 256, 256], P(None, 'gz', 'gy', 'gx')
- temperature_new: float32 [4, 256, 256], P('gz', 'gy', 'gx')
- salinity_new: float32 [8, 512, 512], P('gz', ('gx', 'gy'))
The draws below stay inside these ranges and needn't reach their ends.
All inputs are finite; a program needn't handle non-finite values.
Results may differ from the reference program's by a relative error of at most 0.00002.
Values sent between devices are 32-bit elements; how exact they have to be, the bound alone decides.
A program may use at most 128 MiB of HBM per device.

```python
import jax
import jax.numpy as jnp
from jax import lax

LOWRES_DEPTHS = 4
LOWRES_SPAN_X = 256
LOWRES_SPAN_Y = 256


def block_scale(stream_key, shape, cuts, least, high):
    loudness, own = 1.0, jax.random.fold_in(stream_key, 6)
    for position, shards_of in cuts:
        steps = jnp.exp(jax.random.uniform(jax.random.fold_in(own, position), (shards_of,), jnp.float32, least / len(cuts), high / len(cuts)))
        loudness = loudness * jnp.repeat(steps, shape[position] // shards_of).reshape([-1 if axis == position else 1 for axis in range(len(shape))])
    return loudness


def scatter_about(stream_key, shape, width, most, split=(), dtype=jnp.bfloat16):
    loudness = block_scale(stream_key, shape, split, -0.22, 0.18) if split else 1.0
    entries = jax.random.normal(stream_key, shape, jnp.float32) * width * loudness
    return jnp.minimum(jnp.maximum(entries, -most), most).astype(dtype)


def setup_inputs(seed: int = 0) -> dict:
    key_list = jax.random.split(jax.random.key(seed), 4)
    return {
        "flow_vector_lowres": scatter_about(key_list[0], (3, LOWRES_DEPTHS, LOWRES_SPAN_X, LOWRES_SPAN_Y), 0.5, 3.0, ((1, 2), (2, 8), (3, 2)), jnp.float32),
        "heat_anomaly_lowres": scatter_about(key_list[1], (LOWRES_DEPTHS, LOWRES_SPAN_X, LOWRES_SPAN_Y), 1.0, 6.0, ((0, 2), (1, 8), (2, 2)), jnp.float32),
        "salt_content_anomaly": scatter_about(key_list[2], (2 * LOWRES_DEPTHS, 2 * LOWRES_SPAN_Y, 2 * LOWRES_SPAN_X), 1.0, 6.0, ((0, 2), (1, 16)), jnp.float32),
    }


time_step = 0.1
viscosity = 0.2
heat_diffusion = 0.15
salt_diffusion = 0.05
expansion = 1.0
thermal_expansion_curve = 0.5
contraction = 0.8
even_weights = (-0.0390625, 0.2734375, 0.8203125, -0.0546875)
odd_weights = (-0.0546875, 0.8203125, 0.2734375, -0.0390625)


def refine(padded, along_dim):
    length = padded.shape[along_dim] - 4
    even_part = even_weights[0] * lax.slice_in_dim(padded, 0, length, axis=along_dim)
    odd_part = odd_weights[0] * lax.slice_in_dim(padded, 1, length + 1, axis=along_dim)
    for offset in range(1, 4):
        even_part = even_part + even_weights[offset] * lax.slice_in_dim(padded, offset, offset + length, axis=along_dim)
        odd_part = odd_part + odd_weights[offset] * lax.slice_in_dim(padded, offset + 1, offset + 1 + length, axis=along_dim)
    target = list(even_part.shape)
    target[along_dim] = 2 * length
    return jnp.stack([even_part, odd_part], axis=along_dim + 1).reshape(target)


def window(padded, target, along_dim, offset):
    leading = padded.ndim - 3
    starts = [0] * leading + [1, 1, 1]
    starts[leading + along_dim] = offset
    limits = [start_at + extent for start_at, extent in zip(starts, target)]
    return lax.slice(padded, starts, limits)


def tendency(field, padded, speeds, spacing, diffusion):
    advection = jnp.zeros(field.shape, jnp.float32)
    neighbours = jnp.zeros(field.shape, jnp.float32)
    for along_dim in range(3):
        below_cells = window(padded, field.shape, along_dim, 0)
        above_cells = window(padded, field.shape, along_dim, 2)
        advect_speed = speeds[along_dim]
        advection = advection + jnp.maximum(advect_speed, 0.0) * (field - below_cells) + jnp.minimum(advect_speed, 0.0) * (above_cells - field)
        neighbours = neighbours + below_cells + above_cells
    return diffusion * (neighbours - 6.0 * field) / (spacing * spacing) - advection / spacing


def coarse_rates(prognostic_variables, padded, buoyancy):
    diffusion = jnp.array([viscosity, viscosity, viscosity, heat_diffusion], jnp.float32).reshape(4, 1, 1, 1)
    coarse_tendency_rate = tendency(prognostic_variables, padded, (prognostic_variables[0], prognostic_variables[1], prognostic_variables[2]), 1.0, diffusion)
    return jnp.concatenate([coarse_tendency_rate[:1] + buoyancy[None], coarse_tendency_rate[1:]], axis=0)


def restrict(refined_field):
    level_count = refined_field.shape[0]
    row_count = refined_field.shape[1]
    col_count = refined_field.shape[2]
    grouped = refined_field.reshape(level_count // 2, 2, row_count // 2, 2, col_count // 2, 2)
    return 0.125 * jnp.sum(grouped, axis=(1, 3, 5))


def fine_rates(refined, salt_content_anomaly, salt_padded):
    salt_rate = tendency(salt_content_anomaly, salt_padded, (refined[0], refined[2], refined[1]), 0.5, salt_diffusion)
    buoyant = expansion * refined[3] * (1.0 + thermal_expansion_curve * refined[3]) - contraction * salt_content_anomaly
    return salt_rate, restrict(buoyant)


def heun_rates(prognostic_variables, salt_content_anomaly):
    turned = jnp.transpose(prognostic_variables, (0, 1, 3, 2))
    padded = jnp.pad(turned, ((0, 0), (2, 2), (2, 2), (2, 2)))
    refined = refine(refine(refine(padded, 1), 2), 3)
    salt_rate, coarse_buoyancy = fine_rates(refined, salt_content_anomaly, jnp.pad(salt_content_anomaly, 1))
    near_rim = jnp.pad(prognostic_variables, ((0, 0), (1, 1), (1, 1), (1, 1)))
    return coarse_rates(prognostic_variables, near_rim, jnp.transpose(coarse_buoyancy, (0, 2, 1))), salt_rate


def reference(flow_vector_lowres, heat_anomaly_lowres, salt_content_anomaly):
    prognostic_variables = jnp.concatenate([flow_vector_lowres, heat_anomaly_lowres[None]], axis=0)
    coarse_tendency_rate, salt_rate = heun_rates(prognostic_variables, salt_content_anomaly)
    fields_mid = prognostic_variables + time_step * coarse_tendency_rate
    salt_mid = salt_content_anomaly + time_step * salt_rate
    coarse_rate_mid, salt_rate_mid = heun_rates(fields_mid, salt_mid)
    fields_end = 0.5 * prognostic_variables + 0.5 * (fields_mid + time_step * coarse_rate_mid)
    salt_end = 0.5 * salt_content_anomaly + 0.5 * (salt_mid + time_step * salt_rate_mid)
    return fields_end[:3], fields_end[3], salt_end
```

```python
import functools

import jax
import jax.numpy as jnp
from jax import lax
from jax.experimental import pallas as pl
from jax.experimental.pallas import tpu as pltpu
from jax.sharding import PartitionSpec as P

time_step = 0.1
viscosity = 0.2
heat_diffusion = 0.15
salt_diffusion = 0.05
expansion = 1.0
thermal_expansion_curve = 0.5
contraction = 0.8
even_weights = (-0.0390625, 0.2734375, 0.8203125, -0.0546875)
odd_weights = (-0.0546875, 0.8203125, 0.2734375, -0.0390625)
diffusion = (viscosity, viscosity, viscosity, heat_diffusion)
OFF = 8
WIDE = 4


def split_dot(value, matrix, dims):
    rows = value.shape[0]
    high = value.astype(jnp.bfloat16)
    rest = value - high.astype(jnp.float32)
    middle = rest.astype(jnp.bfloat16)
    low = (rest - middle.astype(jnp.float32)).astype(jnp.bfloat16)
    stacked = jnp.concatenate([high, middle, low], axis=0)
    out = lax.dot_general(stacked, matrix, (dims, ((), ())), preferred_element_type=jnp.float32)
    return out[:rows] + (out[rows : 2 * rows] + out[2 * rows :])


def taps(weights, values):
    total = weights[0] * values[0]
    for weight, value in zip(weights[1:], values[1:]):
        total = total + weight * value
    return total


def advect(speed, centre, below, above):
    return jnp.maximum(speed, 0.0) * (centre - below) + jnp.minimum(speed, 0.0) * (above - centre)


def kernel(
    ngx, n, nr, nc, cx, ny,
    flow, heat, salt, vel_out, heat_out, salt_out,
    turned, message, edge, got, got_edge, fields, mids, cols, cols_mid, warm, fine,
    grains, grains_mid, mean_salt, buoy, outgoing, landed, fold, widen,
    main_send, main_recv, pass_send, edge_send, edge_recv, mean_send, mean_recv,
    rim_send, rim_recv, end_send, end_recv,
):
    gx, gy, gz = lax.axis_index("gx"), lax.axis_index("gy"), lax.axis_index("gz")
    other = 1 - gz
    r = gx * n + gy
    last = ngx * n - 1
    frame = nr + 2 * WIDE
    padded = nr + 2 * OFF
    f32 = jnp.float32

    def at(x, y, z):
        return {"gx": x, "gy": y, "gz": z}

    up_x, up_y = jnp.where(gy == n - 1, gx + 1, gx), jnp.where(gy == n - 1, 0, gy + 1)
    dn_x, dn_y = jnp.where(gy == 0, gx - 1, gx), jnp.where(gy == 0, n - 1, gy - 1)

    barrier = pltpu.get_barrier_semaphore()

    def greet(x, y, z):
        pl.semaphore_signal(barrier, inc=1, device_id=at(x, y, z), device_id_type=pl.DeviceIdType.MESH)

    for d in range(1, n):
        greet(gx, lax.rem(gy + d, n), gz)
    greet(gx, gy, other)

    @pl.when(r > 0)
    def _():
        greet(dn_x, dn_y, gz)
        greet(dn_x, dn_y, other)

    @pl.when(r < last)
    def _():
        greet(up_x, up_y, gz)
        greet(up_x, up_y, other)

    takes_low = jnp.logical_and(gy == 0, gx > 0)
    takes_high = jnp.logical_and(gy == n - 1, gx < ngx - 1)

    @pl.when(takes_low)
    def _():
        for j in range(n):
            for z in range(2):
                greet(gx - 1, j, z)

    @pl.when(takes_high)
    def _():
        for j in range(n):
            for z in range(2):
                greet(gx + 1, j, z)

    tile = jnp.concatenate([flow[...].reshape(6 * cx, ny), heat[...].reshape(2 * cx, ny)], axis=0)
    lanes = 8 * cx
    zero8 = jnp.zeros((8, lanes), f32)
    turned[0:8] = zero8
    turned[8 + ny : 16 + ny] = zero8
    turned[8 : 8 + ny] = tile.T
    for j in range(n):
        base = 8 + nr * j
        message[j, 0:nr] = turned[base : base + nr]
        message[j, nr : nr + 4] = turned[base + nr : base + nr + 4]
        message[j, nr + 4 : nr + 8] = turned[base - 4 : base]
    edge[0, 0:4] = zero8[:4]
    edge[0, 4:8] = turned[4 + ny : 8 + ny]
    edge[1, 0:4] = turned[8:12]
    edge[1, 4:8] = zero8[:4]

    lowers = jnp.where(gx > 0, 2, 0)
    highers = jnp.where(gx < ngx - 1, 2, 0)
    sides = jnp.where(r > 0, 2, 0) + jnp.where(r < last, 2, 0)
    pl.semaphore_wait(barrier, n + sides + lowers + highers)

    def remote(src, dst, send, recv, x, y, z):
        return pltpu.make_async_remote_copy(
            src_ref=src, dst_ref=dst, send_sem=send, recv_sem=recv,
            device_id=at(x, y, z), device_id_type=pl.DeviceIdType.MESH,
        )

    main = []
    for d in range(1, n):
        to = lax.rem(gy + d, n)
        main.append(remote(message.at[to], got.at[gz, gy], main_send.at[d], main_recv.at[gz, gy], gx, to, gz))
        main[-1].start()

    def passed(j, z):
        return remote(got.at[z, j], got.at[z, j], pass_send.at[j], main_recv.at[z, j], gx, gy, other)

    got[gz, gy] = message[gy]
    passed(gy, gz).start()

    def edge_copy(which, z):
        x = gx + 1 if which == 0 else gx - 1
        y = 0 if which == 0 else n - 1
        return remote(edge.at[which], got_edge.at[gz, gy], edge_send.at[which, z], edge_recv.at[gz, gy], x, y, z)

    @pl.when(gx < ngx - 1)
    def _():
        for z in range(2):
            edge_copy(0, z).start()

    @pl.when(gx > 0)
    def _():
        for z in range(2):
            edge_copy(1, z).start()

    takes_edge = jnp.logical_or(takes_low, takes_high)

    @pl.when(jnp.logical_not(takes_edge))
    def _():
        got_edge[...] = jnp.zeros(got_edge.shape, f32)

    row_id = lax.broadcasted_iota(jnp.int32, (2 * nc, 2 * nc), 0)
    col_id = lax.broadcasted_iota(jnp.int32, (2 * nc, 2 * nc), 1)
    source = jnp.where(col_id < nc, 2 * col_id, 2 * (col_id - nc) + 1)
    fold[...] = jnp.where(row_id == source, 1.0, 0.0).astype(jnp.bfloat16)
    parts = []
    for lf in range(4):
        for rp in range(2):
            parts.append(
                jnp.concatenate(
                    [salt[lf, c, pl.ds(rp, nr, stride=2), :] for c in range(nc // 64)], axis=1
                )
            )
    folded = split_dot(jnp.concatenate(parts, axis=0), fold[...], ((1,), (0,)))
    for lf in range(4):
        for rp in range(2):
            k = (lf * 2 + rp) * nr
            grains[lf + 1, rp, OFF : OFF + nr] = folded[k : k + nr]

    def walls(buf):
        @pl.when(gz == 0)
        def _():
            buf[0] = jnp.zeros(buf.shape[1:], f32)

        @pl.when(gz == 1)
        def _():
            buf[5] = jnp.zeros(buf.shape[1:], f32)

        @pl.when(r == 0)
        def _():
            buf[1:5, 1, 0:OFF] = jnp.zeros((4, OFF, 2 * nc), f32)

        @pl.when(r == last)
        def _():
            buf[1:5, 0, OFF + nr : padded] = jnp.zeros((4, OFF, 2 * nc), f32)

    own = pl.ds(OFF, nr)

    def rims(buf, s):
        down = remote(
            buf.at[1:5, 0, OFF : OFF + 8], buf.at[1:5, 0, OFF + nr : padded],
            rim_send.at[s, 1], rim_recv.at[s, 1], dn_x, dn_y, gz,
        )
        up = remote(
            buf.at[1:5, 1, nr : OFF + nr], buf.at[1:5, 1, 0:OFF],
            rim_send.at[s, 2], rim_recv.at[s, 2], up_x, up_y, gz,
        )
        return down, up

    def rim_start(buf, s):
        down, up = rims(buf, s)
        level_copy(buf, s).start()

        @pl.when(r > 0)
        def _():
            down.start()

        @pl.when(r < last)
        def _():
            up.start()

    def level_copy(buf, s):
        return remote(
            buf.at[4 - 3 * gz, :, own], buf.at[5 * gz, :, own], rim_send.at[s, 0], rim_recv.at[s, 0], gx, gy, other
        )

    def level_landed(buf, s):
        return remote(
            buf.at[4 - 3 * gz, :, own], buf.at[5 * (1 - gz), :, own], rim_send.at[s, 0], rim_recv.at[s, 0], gx, gy, other
        )

    def rim_wait(buf, s):
        down, up = rims(buf, s)
        level_landed(buf, s).wait_recv()
        level_copy(buf, s).wait_send()

        @pl.when(r > 0)
        def _():
            up.wait_recv()
            down.wait_send()

        @pl.when(r < last)
        def _():
            down.wait_recv()
            up.wait_send()

    walls(grains)
    rim_start(grains, 0)

    def halves(value):
        return value[:, :nc] + value[:, nc:]

    for l in range(2):
        total = sum(grains[1 + 2 * l + p, q, OFF : OFF + nr] for p in range(2) for q in range(2))
        mean_salt[gz * 2 + l, OFF : OFF + nr] = 0.125 * halves(total)

    @pl.when(r == 0)
    def _():
        mean_salt[:, 0:OFF] = jnp.zeros((4, OFF, nc), f32)

    @pl.when(r == last)
    def _():
        mean_salt[:, OFF + nr : padded] = jnp.zeros((4, OFF, nc), f32)

    def mean_copy(k):
        mine = pl.ds(gz * 2, 2)
        if k == 0:
            part = mean_salt.at[mine, OFF : OFF + nr]
            return remote(part, part, mean_send.at[0], mean_recv.at[0], gx, gy, other)
        z = gz if k % 2 else other
        if k < 3:
            return remote(
                mean_salt.at[mine, nr : OFF + nr], mean_salt.at[mine, 0:OFF],
                mean_send.at[k], mean_recv.at[k], up_x, up_y, z,
            )
        return remote(
            mean_salt.at[mine, OFF : OFF + 8], mean_salt.at[mine, OFF + nr : padded],
            mean_send.at[k], mean_recv.at[k], dn_x, dn_y, z,
        )

    def mean_landed(k):
        from_z = gz if k % 2 else other
        theirs = pl.ds(from_z * 2, 2)
        if k == 0:
            part = mean_salt.at[theirs, OFF : OFF + nr]
        elif k < 3:
            part = mean_salt.at[theirs, 0:OFF]
        else:
            part = mean_salt.at[theirs, OFF + nr : padded]
        return remote(part, part, mean_send.at[k], mean_recv.at[k], gx, gy, other)

    mean_copy(0).start()

    @pl.when(r < last)
    def _():
        mean_copy(1).start()
        mean_copy(2).start()

    @pl.when(r > 0)
    def _():
        mean_copy(3).start()
        mean_copy(4).start()

    for d in range(1, n):
        j = lax.rem(gy + n - d, n)
        passed(j, gz).wait_recv()
        passed(j, gz).start()

    row_id = lax.broadcasted_iota(jnp.int32, (nc, 2 * nc), 0)
    col_id = lax.broadcasted_iota(jnp.int32, (nc, 2 * nc), 1)
    odd = col_id >= nc
    step = row_id - jnp.where(odd, col_id - nc - 1, col_id - 2)
    band = jnp.zeros((nc, 2 * nc), f32)
    for k in range(4):
        band = jnp.where(step == k, jnp.where(odd, odd_weights[k], even_weights[k]), band)
    widen[...] = band.astype(jnp.bfloat16)

    for buf in (cols, cols_mid):
        for f in range(4):
            for level in (0, 1, 6, 7):
                buf[f, level] = jnp.zeros((padded, 2 * nc), f32)
    for f in range(4):
        for level in (0, 5):
            fields[f, level] = jnp.zeros((padded, nc), f32)
            mids[f, level] = jnp.zeros((padded, nc), f32)

    @pl.when(takes_edge)
    def _():
        for z in range(2):
            for j in range(n):
                remote(edge.at[0], got_edge.at[z, j], edge_send.at[0, 0], edge_recv.at[z, j], gx, gy, other).wait_recv()

    chunk = lax.broadcasted_iota(jnp.int32, (nr + 8, 128), 1) // cx
    per = 128 // cx

    def gather_chunks(values, k):
        out = None
        for j, value in enumerate(values):
            shift = (cx * (j - k)) % 128
            moved = pltpu.roll(value, shift, axis=1) if shift else value
            out = moved if out is None else jnp.where(chunk[: value.shape[0]] == j, moved, out)
        return out

    def assemble(z):
        for t in range(lanes // 128):
            for a in range(n // per):
                values = []
                for j in range(per):
                    body = got[z, per * a + j, 0:nr, 128 * t : 128 * (t + 1)]
                    rim = (
                        got[z, per * a + j, nr : nr + 8, 128 * t : 128 * (t + 1)]
                        + got_edge[z, per * a + j, :, 128 * t : 128 * (t + 1)]
                    )
                    values.append(jnp.concatenate([body, rim], axis=0))
                for k in range(per):
                    pair = per * t + k
                    f, l = pair // 2, pair % 2
                    whole = gather_chunks(values, k)
                    where = slice(128 * a, 128 * (a + 1))
                    level = z * 2 + l + 1
                    fields[f, level, OFF : OFF + nr, where] = whole[:nr]
                    fields[f, level, 0:8, where] = whole[nr:]
                    fields[f, level, OFF + nr : padded, where] = whole[nr:]

    assemble(gz)
    for d in range(n):
        j = lax.rem(gy + d, n)
        passed(j, other).wait_recv()
    assemble(other)

    def widen_all(src, dst):
        for f in range(4):
            stack = src[f, 1:5].reshape(4 * padded, nc)
            wide = split_dot(stack, widen[...], ((1,), (0,)))
            for level in range(4):
                dst[f, level + 2] = wide[level * padded : (level + 1) * padded]

    widen_all(fields, cols)

    def level_taps(buf, f, base, lf):
        i, p = base + lf // 2, lf % 2
        return taps((even_weights, odd_weights)[p], [buf[f, i + k + p] for k in range(4)])

    def row_taps(read, start, count, rp):
        return taps((even_weights, odd_weights)[rp], [read(start - 2 + k + rp, count) for k in range(4)])

    def warm_mean(count, start, pick, l):
        total = None
        for lp in range(2):
            for rp in range(2):
                x = row_taps(lambda s, c: pick(2 * l + lp, s, c), start, count, rp)
                x = expansion * x * (1.0 + thermal_expansion_curve * x)
                total = x if total is None else total + x
        return 0.125 * halves(total)

    lo = OFF - WIDE

    for f in range(3):
        for lf in range(4):
            fine[f, lf] = level_taps(cols, f, 2 * gz, lf)

    rim_wait(grains, 0)
    lane = lax.broadcasted_iota(jnp.int32, (nr, nc), 1)

    def salt_rate(buf, lf, rp):
        centre = buf[lf + 1, rp, OFF : OFF + nr]
        lower, upper = buf[lf, rp, OFF : OFF + nr], buf[lf + 2, rp, OFF : OFF + nr]
        if rp == 0:
            before, after = buf[lf + 1, 1, OFF - 1 : OFF - 1 + nr], buf[lf + 1, 1, OFF : OFF + nr]
        else:
            before, after = buf[lf + 1, 0, OFF : OFF + nr], buf[lf + 1, 0, OFF + 1 : OFF + 1 + nr]
        even, uneven = centre[:, :nc], centre[:, nc:]
        left = jnp.concatenate([jnp.where(lane == 0, 0.0, pltpu.roll(uneven, 1, axis=1)), even], axis=1)
        right = jnp.concatenate([uneven, jnp.where(lane == nc - 1, 0.0, pltpu.roll(even, nc - 1, axis=1))], axis=1)
        w, u, v = [row_taps(lambda s, c: fine[f, lf, s : s + c], OFF, nr, rp) for f in range(3)]
        flux = advect(w, centre, lower, upper) + advect(v, centre, before, after) + advect(u, centre, left, right)
        around = (lower + upper) + (before + after) + (left + right)
        return centre, (4.0 * salt_diffusion) * (around - 6.0 * centre) - 2.0 * flux

    mean_mid = []
    for l in range(2):
        total = None
        for lf in (2 * l, 2 * l + 1):
            for rp in range(2):
                centre, rate = salt_rate(grains, lf, rp)
                mid = centre + time_step * rate
                grains_mid[lf + 1, rp, OFF : OFF + nr] = mid
                total = mid if total is None else total + mid
        mean_mid.append(0.125 * halves(total))
    walls(grains_mid)
    rim_start(grains_mid, 1)

    for lf in range(8):
        warm[lf] = level_taps(cols, 3, 0, lf)
    mean_landed(0).wait_recv()

    @pl.when(r > 0)
    def _():
        mean_landed(1).wait_recv()
        mean_landed(2).wait_recv()

    @pl.when(r < last)
    def _():
        mean_landed(3).wait_recv()
        mean_landed(4).wait_recv()

    for l in range(4):
        heat_part = warm_mean(frame, lo, lambda i, s, c: warm[i, s : s + c], l)
        buoy[l] = heat_part - contraction * mean_salt[l, lo : lo + frame]

    def coarse_step(buf, level, start, count, lift):
        here = lax.broadcasted_iota(jnp.int32, (count, nc), 1)
        rows = pl.ds(start, count)
        centres = [buf[f, level, rows] for f in range(4)]
        out = []
        for f in range(4):
            q = centres[f]
            lower, upper = buf[f, level - 1, rows], buf[f, level + 1, rows]
            before, after = buf[f, level, start - 1 : start - 1 + count], buf[f, level, start + 1 : start + 1 + count]
            left = jnp.where(here == 0, 0.0, pltpu.roll(q, 1, axis=1))
            right = jnp.where(here == nc - 1, 0.0, pltpu.roll(q, nc - 1, axis=1))
            flux = (
                advect(centres[0], q, lower, upper)
                + advect(centres[1], q, left, right)
                + advect(centres[2], q, before, after)
            )
            around = (lower + upper) + (before + after) + (left + right)
            rate = diffusion[f] * (around - 6.0 * q) - flux
            out.append((q, rate + lift if f == 0 else rate))
        return out

    row = lax.broadcasted_iota(jnp.int32, (frame, nc), 0) + (r * nr - WIDE)
    inside = jnp.logical_and(row >= 0, row < (last + 1) * nr)
    for f in range(4):
        for level in range(4):
            mids[f, level + 1, 0:8] = jnp.zeros((8, nc), f32)
            mids[f, level + 1, OFF + nr : padded] = jnp.zeros((8, nc), f32)
    for level in range(4):
        for f, (q, rate) in enumerate(coarse_step(fields, level + 1, lo, frame, buoy[level])):
            mids[f, level + 1, lo : lo + frame] = jnp.where(inside, q + time_step * rate, 0.0)

    widen_all(mids, cols_mid)
    for lf in range(4):
        warm[lf] = level_taps(cols_mid, 3, 2 * gz, lf)
    results = []
    for l in range(2):
        lift = warm_mean(nr, OFF, lambda i, s, c: warm[i, s : s + c], l) - contraction * mean_mid[l]
        level = gz * 2 + l + 1
        steps = coarse_step(mids, level, OFF, nr, lift)
        results.append(
            [0.5 * fields[f, level, OFF : OFF + nr] + 0.5 * (q + time_step * rate) for f, (q, rate) in enumerate(steps)]
        )
    for a in range(n // per):
        for t in range(lanes // 128):
            values = []
            for k in range(per):
                pair = per * t + k
                values.append(results[pair % 2][pair // 2][:, 128 * a : 128 * (a + 1)])
            for j in range(per):
                outgoing[per * a + j, :, 128 * t : 128 * (t + 1)] = gather_chunks(values, j)
    ends = []
    for d in range(1, n):
        to = lax.rem(gy + d, n)
        ends.append(remote(outgoing.at[to], landed.at[gy], end_send.at[d], end_recv.at[gy], gx, to, gz))
        ends[-1].start()
    landed[gy] = outgoing[gy]

    for f in range(3):
        for lf in range(4):
            fine[f, lf] = level_taps(cols_mid, f, 2 * gz, lf)
    rim_wait(grains_mid, 1)
    parts = []
    for lf in range(4):
        for rp in range(2):
            centre, rate = salt_rate(grains_mid, lf, rp)
            parts.append(0.5 * grains[lf + 1, rp, OFF : OFF + nr] + 0.5 * (centre + time_step * rate))
    whole = split_dot(jnp.concatenate(parts, axis=0), fold[...], ((1,), (1,)))
    for lf in range(4):
        for rp in range(2):
            k = (lf * 2 + rp) * nr
            for c in range(nc // 64):
                salt_out[lf, c, pl.ds(rp, nr, stride=2), :] = whole[k : k + nr, 128 * c : 128 * (c + 1)]

    for d in range(1, n):
        j = lax.rem(gy + n - d, n)
        remote(outgoing.at[j], landed.at[j], end_send.at[d], end_recv.at[j], gx, j, gz).wait_recv()
    back = landed[...].reshape(ny, lanes).T
    vel_out[...] = back[: 6 * cx].reshape(3, 2, cx, ny)
    heat_out[...] = back[6 * cx :].reshape(2, cx, ny)

    for copy in main + ends:
        copy.wait_send()
    for j in range(n):
        passed(j, gz).wait_send()
    mean_copy(0).wait_send()

    @pl.when(gx < ngx - 1)
    def _():
        for z in range(2):
            edge_copy(0, z).wait_send()

    @pl.when(gx > 0)
    def _():
        for z in range(2):
            edge_copy(1, z).wait_send()

    @pl.when(r < last)
    def _():
        mean_copy(1).wait_send()
        mean_copy(2).wait_send()

    @pl.when(r > 0)
    def _():
        mean_copy(3).wait_send()
        mean_copy(4).wait_send()


def on_device(ngx, n, flow, heat, salt):
    cx, ny = flow.shape[2], flow.shape[3]
    nr, nc = salt.shape[1] // 2, salt.shape[2] // 2
    padded = nr + 2 * OFF
    lanes = 8 * cx
    f32, dma = jnp.float32, pltpu.SemaphoreType.DMA
    vmem = pl.BlockSpec(memory_space=pltpu.VMEM)
    split = salt.reshape(4, 2 * nr, nc // 64, 128).transpose(0, 2, 1, 3)
    vel, temp, out = pl.pallas_call(
        functools.partial(kernel, ngx, n, nr, nc, cx, ny),
        out_shape=(
            jax.ShapeDtypeStruct(flow.shape, f32),
            jax.ShapeDtypeStruct(heat.shape, f32),
            jax.ShapeDtypeStruct(split.shape, f32),
        ),
        in_specs=[vmem] * 3,
        out_specs=(vmem,) * 3,
        scratch_shapes=[
            pltpu.VMEM((ny + 16, lanes), f32),
            pltpu.VMEM((n, nr + 8, lanes), f32),
            pltpu.VMEM((2, 8, lanes), f32),
            pltpu.VMEM((2, n, nr + 8, lanes), f32),
            pltpu.VMEM((2, n, 8, lanes), f32),
            pltpu.VMEM((4, 6, padded, nc), f32),
            pltpu.VMEM((4, 6, padded, nc), f32),
            pltpu.VMEM((4, 8, padded, 2 * nc), f32),
            pltpu.VMEM((4, 8, padded, 2 * nc), f32),
            pltpu.VMEM((8, padded, 2 * nc), f32),
            pltpu.VMEM((3, 4, padded, 2 * nc), f32),
            pltpu.VMEM((6, 2, padded, 2 * nc), f32),
            pltpu.VMEM((6, 2, padded, 2 * nc), f32),
            pltpu.VMEM((4, padded, nc), f32),
            pltpu.VMEM((4, nr + 2 * WIDE, nc), f32),
            pltpu.VMEM((n, nr, lanes), f32),
            pltpu.VMEM((n, nr, lanes), f32),
            pltpu.VMEM((2 * nc, 2 * nc), jnp.bfloat16),
            pltpu.VMEM((nc, 2 * nc), jnp.bfloat16),
            dma((n,)), dma((2, n)), dma((n,)), dma((2, 2)), dma((2, n)), dma((5,)), dma((5,)),
            dma((2, 3)), dma((2, 3)), dma((n,)), dma((n,)),
        ],
        compiler_params=pltpu.CompilerParams(
            collective_id=0, has_side_effects=True, vmem_limit_bytes=48 * 1024 * 1024
        ),
    )(flow, heat, split)
    return vel, temp, out.transpose(0, 2, 1, 3).reshape(salt.shape)


def solution(mesh):
    in_specs = (P(None, "gz", "gy", "gx"), P("gz", "gy", "gx"), P("gz", ("gx", "gy"), None))
    out_specs = (P(None, "gz", "gy", "gx"), P("gz", "gy", "gx"), P("gz", ("gx", "gy"), None))
    return jax.shard_map(
        functools.partial(on_device, mesh.shape["gx"], mesh.shape["gy"]),
        mesh=mesh, in_specs=in_specs, out_specs=out_specs, check_vma=False,
    )
```

```python
import functools

import jax
import jax.numpy as jnp
from jax import lax
from jax.experimental import pallas as pl
from jax.experimental.pallas import tpu as pltpu
from jax.sharding import PartitionSpec as P

time_step = 0.1
viscosity = 0.2
heat_diffusion = 0.15
salt_diffusion = 0.05
expansion = 1.0
thermal_expansion_curve = 0.5
contraction = 0.8
even_weights = (-0.0390625, 0.2734375, 0.8203125, -0.0546875)
odd_weights = (-0.0546875, 0.8203125, 0.2734375, -0.0390625)
diffusion = (viscosity, viscosity, viscosity, heat_diffusion)
VMEM = 64 * 1024 * 1024
OFF = 8
WIDE = 4


def split_dot(value, matrix, dims, count=3):
    rows = value.shape[0]
    parts = []
    for k in range(count):
        parts.append(value.astype(jnp.bfloat16))
        if k < count - 1:
            value = value - parts[-1].astype(jnp.float32)
    stacked = jnp.concatenate(parts, axis=0)
    out = lax.dot_general(stacked, matrix, (dims, ((), ())), preferred_element_type=jnp.float32)
    total = out[(count - 1) * rows :]
    for k in range(count - 2, -1, -1):
        total = out[k * rows : (k + 1) * rows] + total
    return total


def taps(weights, values):
    total = weights[0] * values[0]
    for weight, value in zip(weights[1:], values[1:]):
        total = total + weight * value
    return total


def advect(speed, centre, below, above):
    return jnp.maximum(speed, 0.0) * (centre - below) + jnp.minimum(speed, 0.0) * (above - centre)


def kernel(
    ngx, n, nr, nc, cx, ny,
    flow_in, heat_in, salt_in, vel_out, heat_out, salt_out,
    flow, heat, salt, turned, message, edge, got, got_edge, fields, mids, tall, fine,
    grains, grains_mid, mean_salt, buoy, outgoing, landed, fold, widen,
    main_send, main_recv, pass_send, edge_send, edge_recv, mean_send, mean_recv,
    rim_send, rim_recv, end_send, end_recv, load,
):
    gx, gy, gz = lax.axis_index("gx"), lax.axis_index("gy"), lax.axis_index("gz")
    other = 1 - gz
    r = gx * n + gy
    last = ngx * n - 1
    frame = nr + 2 * WIDE
    padded = nr + 2 * OFF
    f32 = jnp.float32

    def at(x, y, z):
        return {"gx": x, "gy": y, "gz": z}

    up_x, up_y = jnp.where(gy == n - 1, gx + 1, gx), jnp.where(gy == n - 1, 0, gy + 1)
    dn_x, dn_y = jnp.where(gy == 0, gx - 1, gx), jnp.where(gy == 0, n - 1, gy - 1)

    loads = [pltpu.make_async_copy(flow_in, flow, load.at[0]), pltpu.make_async_copy(heat_in, heat, load.at[1])]
    for c in range(nc // 64):
        loads.append(
            pltpu.make_async_copy(salt_in.at[:, :, 128 * c : 128 * (c + 1)], salt.at[:, c], load.at[2 + c])
        )
    for copy in loads:
        copy.start()

    barrier = pltpu.get_barrier_semaphore()

    def greet(x, y, z):
        pl.semaphore_signal(barrier, inc=1, device_id=at(x, y, z), device_id_type=pl.DeviceIdType.MESH)

    for d in range(1, n):
        greet(gx, lax.rem(gy + d, n), gz)
    greet(gx, gy, other)

    @pl.when(r > 0)
    def _():
        greet(dn_x, dn_y, gz)
        greet(dn_x, dn_y, other)

    @pl.when(r < last)
    def _():
        greet(up_x, up_y, gz)
        greet(up_x, up_y, other)

    takes_low = jnp.logical_and(gy == 0, gx > 0)
    takes_high = jnp.logical_and(gy == n - 1, gx < ngx - 1)

    @pl.when(takes_low)
    def _():
        for j in range(n):
            for z in range(2):
                greet(gx - 1, j, z)

    @pl.when(takes_high)
    def _():
        for j in range(n):
            for z in range(2):
                greet(gx + 1, j, z)

    loads[0].wait()
    loads[1].wait()
    tile = jnp.concatenate([flow[...].reshape(6 * cx, ny), heat[...].reshape(2 * cx, ny)], axis=0)
    lanes = 8 * cx
    zero8 = jnp.zeros((8, lanes), f32)
    turned[0:8] = zero8
    turned[8 + ny : 16 + ny] = zero8
    turned[8 : 8 + ny] = tile.T
    for j in range(n):
        base = 8 + nr * j
        message[j, 0:nr] = turned[base : base + nr]
        message[j, nr : nr + 4] = turned[base + nr : base + nr + 4]
        message[j, nr + 4 : nr + 8] = turned[base - 4 : base]
    edge[0, 0:4] = zero8[:4]
    edge[0, 4:8] = turned[4 + ny : 8 + ny]
    edge[1, 0:4] = turned[8:12]
    edge[1, 4:8] = zero8[:4]

    lowers = jnp.where(gx > 0, 2, 0)
    highers = jnp.where(gx < ngx - 1, 2, 0)
    sides = jnp.where(r > 0, 2, 0) + jnp.where(r < last, 2, 0)
    pl.semaphore_wait(barrier, n + sides + lowers + highers)

    def remote(src, dst, send, recv, x, y, z):
        return pltpu.make_async_remote_copy(
            src_ref=src, dst_ref=dst, send_sem=send, recv_sem=recv,
            device_id=at(x, y, z), device_id_type=pl.DeviceIdType.MESH,
        )

    main = []
    for d in range(1, n):
        to = lax.rem(gy + d, n)
        main.append(remote(message.at[to], got.at[gz, gy], main_send.at[d], main_recv.at[gz, gy], gx, to, gz))
        main[-1].start()

    def passed(j, z):
        return remote(got.at[z, j], got.at[z, j], pass_send.at[j], main_recv.at[z, j], gx, gy, other)

    got[gz, gy] = message[gy]
    passed(gy, gz).start()

    def edge_copy(which, z):
        x = gx + 1 if which == 0 else gx - 1
        y = 0 if which == 0 else n - 1
        return remote(edge.at[which], got_edge.at[gz, gy], edge_send.at[which, z], edge_recv.at[gz, gy], x, y, z)

    @pl.when(gx < ngx - 1)
    def _():
        for z in range(2):
            edge_copy(0, z).start()

    @pl.when(gx > 0)
    def _():
        for z in range(2):
            edge_copy(1, z).start()

    takes_edge = jnp.logical_or(takes_low, takes_high)

    @pl.when(jnp.logical_not(takes_edge))
    def _():
        got_edge[...] = jnp.zeros(got_edge.shape, f32)

    row_id = lax.broadcasted_iota(jnp.int32, (2 * nc, 2 * nc), 0)
    col_id = lax.broadcasted_iota(jnp.int32, (2 * nc, 2 * nc), 1)
    source = jnp.where(col_id < nc, 2 * col_id, 2 * (col_id - nc) + 1)
    fold[...] = jnp.where(row_id == source, 1.0, 0.0).astype(jnp.bfloat16)
    for copy in loads[2:]:
        copy.wait()
    parts = []
    for lf in range(4):
        for rp in range(2):
            parts.append(
                jnp.concatenate(
                    [salt[lf, c, pl.ds(rp, nr, stride=2), :] for c in range(nc // 64)], axis=1
                )
            )
    folded = split_dot(jnp.concatenate(parts, axis=0), fold[...], ((1,), (0,)))
    for lf in range(4):
        for rp in range(2):
            k = (lf * 2 + rp) * nr
            grains[lf + 1, rp, OFF : OFF + nr] = folded[k : k + nr]

    def walls(buf):
        @pl.when(gz == 0)
        def _():
            buf[0] = jnp.zeros(buf.shape[1:], f32)

        @pl.when(gz == 1)
        def _():
            buf[5] = jnp.zeros(buf.shape[1:], f32)

        @pl.when(r == 0)
        def _():
            buf[1:5, 1, 0:OFF] = jnp.zeros((4, OFF, 2 * nc), f32)

        @pl.when(r == last)
        def _():
            buf[1:5, 0, OFF + nr : padded] = jnp.zeros((4, OFF, 2 * nc), f32)

    own = pl.ds(OFF, nr)

    def rims(buf, s):
        down = remote(
            buf.at[1:5, 0, OFF : OFF + 8], buf.at[1:5, 0, OFF + nr : padded],
            rim_send.at[s, 1], rim_recv.at[s, 1], dn_x, dn_y, gz,
        )
        up = remote(
            buf.at[1:5, 1, nr : OFF + nr], buf.at[1:5, 1, 0:OFF],
            rim_send.at[s, 2], rim_recv.at[s, 2], up_x, up_y, gz,
        )
        return down, up

    def rim_start(buf, s):
        down, up = rims(buf, s)
        level_copy(buf, s).start()

        @pl.when(r > 0)
        def _():
            down.start()

        @pl.when(r < last)
        def _():
            up.start()

    def level_copy(buf, s):
        return remote(
            buf.at[4 - 3 * gz, :, own], buf.at[5 * gz, :, own], rim_send.at[s, 0], rim_recv.at[s, 0], gx, gy, other
        )

    def level_landed(buf, s):
        return remote(
            buf.at[4 - 3 * gz, :, own], buf.at[5 * (1 - gz), :, own], rim_send.at[s, 0], rim_recv.at[s, 0], gx, gy, other
        )

    def rim_wait(buf, s):
        down, up = rims(buf, s)
        level_landed(buf, s).wait_recv()
        level_copy(buf, s).wait_send()

        @pl.when(r > 0)
        def _():
            up.wait_recv()
            down.wait_send()

        @pl.when(r < last)
        def _():
            down.wait_recv()
            up.wait_send()

    walls(grains)
    rim_start(grains, 0)

    def halves(value):
        return value[:, :nc] + value[:, nc:]

    for l in range(2):
        total = sum(grains[1 + 2 * l + p, q, OFF : OFF + nr] for p in range(2) for q in range(2))
        mean_salt[gz * 2 + l, OFF : OFF + nr] = 0.125 * halves(total)

    @pl.when(r == 0)
    def _():
        mean_salt[:, 0:OFF] = jnp.zeros((4, OFF, nc), f32)

    @pl.when(r == last)
    def _():
        mean_salt[:, OFF + nr : padded] = jnp.zeros((4, OFF, nc), f32)

    def mean_copy(k):
        mine = pl.ds(gz * 2, 2)
        if k == 0:
            part = mean_salt.at[mine, OFF : OFF + nr]
            return remote(part, part, mean_send.at[0], mean_recv.at[0], gx, gy, other)
        z = gz if k % 2 else other
        if k < 3:
            return remote(
                mean_salt.at[mine, nr : OFF + nr], mean_salt.at[mine, 0:OFF],
                mean_send.at[k], mean_recv.at[k], up_x, up_y, z,
            )
        return remote(
            mean_salt.at[mine, OFF : OFF + 8], mean_salt.at[mine, OFF + nr : padded],
            mean_send.at[k], mean_recv.at[k], dn_x, dn_y, z,
        )

    def mean_landed(k):
        from_z = gz if k % 2 else other
        theirs = pl.ds(from_z * 2, 2)
        if k == 0:
            part = mean_salt.at[theirs, OFF : OFF + nr]
        elif k < 3:
            part = mean_salt.at[theirs, 0:OFF]
        else:
            part = mean_salt.at[theirs, OFF + nr : padded]
        return remote(part, part, mean_send.at[k], mean_recv.at[k], gx, gy, other)

    mean_copy(0).start()

    @pl.when(r < last)
    def _():
        mean_copy(1).start()
        mean_copy(2).start()

    @pl.when(r > 0)
    def _():
        mean_copy(3).start()
        mean_copy(4).start()

    for d in range(1, n):
        j = lax.rem(gy + n - d, n)
        passed(j, gz).wait_recv()
        passed(j, gz).start()

    row_id = lax.broadcasted_iota(jnp.int32, (nc, 2 * nc), 0)
    col_id = lax.broadcasted_iota(jnp.int32, (nc, 2 * nc), 1)
    odd = col_id >= nc
    step = row_id - jnp.where(odd, col_id - nc - 1, col_id - 2)
    band = jnp.zeros((nc, 2 * nc), f32)
    for k in range(4):
        band = jnp.where(step == k, jnp.where(odd, odd_weights[k], even_weights[k]), band)
    widen[...] = band.astype(jnp.bfloat16)

    for f in range(4):
        for level in (0, 1, 6, 7):
            tall[f, level] = jnp.zeros((2, frame, nc), f32)
    for f in range(4):
        for level in (0, 5):
            fields[f, level] = jnp.zeros((padded, nc), f32)
            mids[f, level] = jnp.zeros((padded, nc), f32)

    @pl.when(takes_edge)
    def _():
        for z in range(2):
            for j in range(n):
                remote(edge.at[0], got_edge.at[z, j], edge_send.at[0, 0], edge_recv.at[z, j], gx, gy, other).wait_recv()

    chunk = lax.broadcasted_iota(jnp.int32, (nr + 8, 128), 1) // cx
    per = 128 // cx

    def gather_chunks(values, k):
        out = None
        for j, value in enumerate(values):
            shift = (cx * (j - k)) % 128
            moved = pltpu.roll(value, shift, axis=1) if shift else value
            out = moved if out is None else jnp.where(chunk[: value.shape[0]] == j, moved, out)
        return out

    def assemble(z):
        for t in range(lanes // 128):
            for a in range(n // per):
                values = []
                for j in range(per):
                    body = got[z, per * a + j, 0:nr, 128 * t : 128 * (t + 1)]
                    rim = (
                        got[z, per * a + j, nr : nr + 8, 128 * t : 128 * (t + 1)]
                        + got_edge[z, per * a + j, :, 128 * t : 128 * (t + 1)]
                    )
                    values.append(jnp.concatenate([body, rim], axis=0))
                for k in range(per):
                    pair = per * t + k
                    f, l = pair // 2, pair % 2
                    whole = gather_chunks(values, k)
                    where = slice(128 * a, 128 * (a + 1))
                    level = z * 2 + l + 1
                    fields[f, level, OFF : OFF + nr, where] = whole[:nr]
                    fields[f, level, 0:8, where] = whole[nr:]
                    fields[f, level, OFF + nr : padded, where] = whole[nr:]

    lo = OFF - WIDE

    def row_taps(buf, f, level, start, count, rp):
        weights = (even_weights, odd_weights)[rp]
        base = start - 2 + rp
        return taps(weights, [buf[f, level, base + k : base + k + count] for k in range(4)])

    def refine_rows(buf, z, start, count):
        for l in range(2):
            level = z * 2 + l
            for rp in range(2):
                for f in range(3):
                    tall[f, level + 2, rp, 0:nr] = row_taps(buf, f, level + 1, OFF, nr, rp)
                tall[3, level + 2, rp, 0:count] = row_taps(buf, 3, level + 1, start, count, rp)

    assemble(gz)
    refine_rows(fields, gz, lo, frame)
    for d in range(n):
        j = lax.rem(gy + d, n)
        passed(j, other).wait_recv()
    assemble(other)
    refine_rows(fields, other, lo, frame)

    def level_taps(f, base, lf, count):
        p = lf % 2
        values, weights = [], []
        for k in range(4):
            level = base + lf // 2 + k + p
            if isinstance(level, int) and not 2 <= level < 6:
                continue
            values.append(tall[f, level, :, 0:count].reshape(2 * count, nc))
            weights.append((even_weights, odd_weights)[p][k])
        return taps(weights, values)

    def widen_pair(f, base, lf, count):
        pair = jnp.concatenate([level_taps(f, base, lf, count), level_taps(f, base, lf + 1, count)], axis=0)
        return split_dot(pair, widen[...], ((1,), (0,)), 2)

    def refine_speeds():
        for f in range(3):
            for lf in (0, 2):
                out = widen_pair(f, 2 * gz, lf, nr)
                for k in range(4):
                    fine[f, lf + k // 2, k % 2] = out[k * nr : (k + 1) * nr]

    def warm_mean(base, l, count):
        x = widen_pair(3, base, 2 * l, count)
        x = expansion * x * (1.0 + thermal_expansion_curve * x)
        return 0.125 * halves(
            (x[:count] + x[count : 2 * count]) + (x[2 * count : 3 * count] + x[3 * count :])
        )

    refine_speeds()
    rim_wait(grains, 0)
    lane = lax.broadcasted_iota(jnp.int32, (nr, nc), 1)

    def salt_rate(buf, lf, rp):
        centre = buf[lf + 1, rp, OFF : OFF + nr]
        lower, upper = buf[lf, rp, OFF : OFF + nr], buf[lf + 2, rp, OFF : OFF + nr]
        if rp == 0:
            before, after = buf[lf + 1, 1, OFF - 1 : OFF - 1 + nr], buf[lf + 1, 1, OFF : OFF + nr]
        else:
            before, after = buf[lf + 1, 0, OFF : OFF + nr], buf[lf + 1, 0, OFF + 1 : OFF + 1 + nr]
        even, uneven = centre[:, :nc], centre[:, nc:]
        left = jnp.concatenate([jnp.where(lane == 0, 0.0, pltpu.roll(uneven, 1, axis=1)), even], axis=1)
        right = jnp.concatenate([uneven, jnp.where(lane == nc - 1, 0.0, pltpu.roll(even, nc - 1, axis=1))], axis=1)
        w, u, v = [fine[f, lf, rp] for f in range(3)]
        flux = advect(w, centre, lower, upper) + advect(v, centre, before, after) + advect(u, centre, left, right)
        around = (lower + upper) + (before + after) + (left + right)
        return centre, (4.0 * salt_diffusion) * (around - 6.0 * centre) - 2.0 * flux

    mean_mid = []
    for l in range(2):
        total = None
        for lf in (2 * l, 2 * l + 1):
            for rp in range(2):
                centre, rate = salt_rate(grains, lf, rp)
                mid = centre + time_step * rate
                grains_mid[lf + 1, rp, OFF : OFF + nr] = mid
                total = mid if total is None else total + mid
        mean_mid.append(0.125 * halves(total))
    walls(grains_mid)
    rim_start(grains_mid, 1)

    mean_landed(0).wait_recv()

    @pl.when(r > 0)
    def _():
        mean_landed(1).wait_recv()
        mean_landed(2).wait_recv()

    @pl.when(r < last)
    def _():
        mean_landed(3).wait_recv()
        mean_landed(4).wait_recv()

    for l in range(4):
        heat_part = warm_mean(0, l, frame)
        buoy[l] = heat_part - contraction * mean_salt[l, lo : lo + frame]

    def coarse_step(buf, level, start, count, lift):
        here = lax.broadcasted_iota(jnp.int32, (count, nc), 1)
        rows = pl.ds(start, count)
        centres = [buf[f, level, rows] for f in range(4)]
        out = []
        for f in range(4):
            q = centres[f]
            lower, upper = buf[f, level - 1, rows], buf[f, level + 1, rows]
            before, after = buf[f, level, start - 1 : start - 1 + count], buf[f, level, start + 1 : start + 1 + count]
            left = jnp.where(here == 0, 0.0, pltpu.roll(q, 1, axis=1))
            right = jnp.where(here == nc - 1, 0.0, pltpu.roll(q, nc - 1, axis=1))
            flux = (
                advect(centres[0], q, lower, upper)
                + advect(centres[1], q, left, right)
                + advect(centres[2], q, before, after)
            )
            around = (lower + upper) + (before + after) + (left + right)
            rate = diffusion[f] * (around - 6.0 * q) - flux
            out.append((q, rate + lift if f == 0 else rate))
        return out

    row = lax.broadcasted_iota(jnp.int32, (frame, nc), 0) + (r * nr - WIDE)
    inside = jnp.logical_and(row >= 0, row < (last + 1) * nr)
    for f in range(4):
        for level in range(4):
            mids[f, level + 1, 0:8] = jnp.zeros((8, nc), f32)
            mids[f, level + 1, OFF + nr : padded] = jnp.zeros((8, nc), f32)
    for level in range(4):
        for f, (q, rate) in enumerate(coarse_step(fields, level + 1, lo, frame, buoy[level])):
            mids[f, level + 1, lo : lo + frame] = jnp.where(inside, q + time_step * rate, 0.0)

    for z in range(2):
        refine_rows(mids, z, OFF, nr)
    results = []
    for l in range(2):
        lift = warm_mean(2 * gz, l, nr) - contraction * mean_mid[l]
        level = gz * 2 + l + 1
        steps = coarse_step(mids, level, OFF, nr, lift)
        results.append(
            [0.5 * fields[f, level, OFF : OFF + nr] + 0.5 * (q + time_step * rate) for f, (q, rate) in enumerate(steps)]
        )
    for a in range(n // per):
        for t in range(lanes // 128):
            values = []
            for k in range(per):
                pair = per * t + k
                values.append(results[pair % 2][pair // 2][:, 128 * a : 128 * (a + 1)])
            for j in range(per):
                outgoing[per * a + j, :, 128 * t : 128 * (t + 1)] = gather_chunks(values, j)
    ends = []
    for d in range(1, n):
        to = lax.rem(gy + d, n)
        ends.append(remote(outgoing.at[to], landed.at[gy], end_send.at[d], end_recv.at[gy], gx, to, gz))
        ends[-1].start()
    landed[gy] = outgoing[gy]

    refine_speeds()
    rim_wait(grains_mid, 1)
    parts = []
    for lf in range(4):
        for rp in range(2):
            centre, rate = salt_rate(grains_mid, lf, rp)
            parts.append(0.5 * grains[lf + 1, rp, OFF : OFF + nr] + 0.5 * (centre + time_step * rate))
    whole = split_dot(jnp.concatenate(parts, axis=0), fold[...], ((1,), (1,)))
    for lf in range(4):
        for rp in range(2):
            k = (lf * 2 + rp) * nr
            for c in range(nc // 64):
                salt[lf, c, pl.ds(rp, nr, stride=2), :] = whole[k : k + nr, 128 * c : 128 * (c + 1)]

    stores = [
        pltpu.make_async_copy(salt.at[:, c], salt_out.at[:, :, 128 * c : 128 * (c + 1)], load.at[2 + c])
        for c in range(nc // 64)
    ]
    for copy in stores:
        copy.start()

    for d in range(1, n):
        j = lax.rem(gy + n - d, n)
        remote(outgoing.at[j], landed.at[j], end_send.at[d], end_recv.at[j], gx, j, gz).wait_recv()
    back = landed[...].reshape(ny, lanes).T
    flow[...] = back[: 6 * cx].reshape(3, 2, cx, ny)
    heat[...] = back[6 * cx :].reshape(2, cx, ny)
    stores += [pltpu.make_async_copy(flow, vel_out, load.at[0]), pltpu.make_async_copy(heat, heat_out, load.at[1])]
    for copy in stores[-2:]:
        copy.start()

    for copy in main + ends:
        copy.wait_send()
    for j in range(n):
        passed(j, gz).wait_send()
    mean_copy(0).wait_send()

    @pl.when(gx < ngx - 1)
    def _():
        for z in range(2):
            edge_copy(0, z).wait_send()

    @pl.when(gx > 0)
    def _():
        for z in range(2):
            edge_copy(1, z).wait_send()

    @pl.when(r < last)
    def _():
        mean_copy(1).wait_send()
        mean_copy(2).wait_send()

    @pl.when(r > 0)
    def _():
        mean_copy(3).wait_send()
        mean_copy(4).wait_send()

    for copy in stores:
        copy.wait()


def store(vel, temp, salt, vel_out, temp_out, salt_out, sems):
    copies = [pltpu.make_async_copy(vel, vel_out, sems.at[0]), pltpu.make_async_copy(temp, temp_out, sems.at[1])]
    for lf in range(4):
        copies.append(pltpu.make_async_copy(salt.at[lf], salt_out.at[lf], sems.at[2 + lf]))
    for copy in copies:
        copy.start()
    for copy in copies:
        copy.wait()


def on_device(ngx, n, flow, heat, salt):
    cx, ny = flow.shape[2], flow.shape[3]
    nr, nc = salt.shape[1] // 2, salt.shape[2] // 2
    padded = nr + 2 * OFF
    lanes = 8 * cx
    f32, dma = jnp.float32, pltpu.SemaphoreType.DMA
    hbm = pl.BlockSpec(memory_space=pltpu.HBM)
    vel, temp, out = pl.pallas_call(
        functools.partial(kernel, ngx, n, nr, nc, cx, ny),
        out_shape=(
            jax.ShapeDtypeStruct(flow.shape, f32),
            jax.ShapeDtypeStruct(heat.shape, f32),
            jax.ShapeDtypeStruct(salt.shape, f32),
        ),
        in_specs=[hbm] * 3,
        out_specs=(hbm,) * 3,
        scratch_shapes=[
            pltpu.VMEM(flow.shape, f32),
            pltpu.VMEM(heat.shape, f32),
            pltpu.VMEM((4, nc // 64, 2 * nr, 128), f32),
            pltpu.VMEM((ny + 16, lanes), f32),
            pltpu.VMEM((n, nr + 8, lanes), f32),
            pltpu.VMEM((2, 8, lanes), f32),
            pltpu.VMEM((2, n, nr + 8, lanes), f32),
            pltpu.VMEM((2, n, 8, lanes), f32),
            pltpu.VMEM((4, 6, padded, nc), f32),
            pltpu.VMEM((4, 6, padded, nc), f32),
            pltpu.VMEM((4, 8, 2, nr + 2 * WIDE, nc), f32),
            pltpu.VMEM((3, 4, 2, nr, 2 * nc), f32),
            pltpu.VMEM((6, 2, padded, 2 * nc), f32),
            pltpu.VMEM((6, 2, padded, 2 * nc), f32),
            pltpu.VMEM((4, padded, nc), f32),
            pltpu.VMEM((4, nr + 2 * WIDE, nc), f32),
            pltpu.VMEM((n, nr, lanes), f32),
            pltpu.VMEM((n, nr, lanes), f32),
            pltpu.VMEM((2 * nc, 2 * nc), jnp.bfloat16),
            pltpu.VMEM((nc, 2 * nc), jnp.bfloat16),
            dma((n,)), dma((2, n)), dma((n,)), dma((2, 2)), dma((2, n)), dma((5,)), dma((5,)),
            dma((2, 3)), dma((2, 3)), dma((n,)), dma((n,)), dma((2 + nc // 64,)),
        ],
        compiler_params=pltpu.CompilerParams(
            collective_id=0, has_side_effects=True, vmem_limit_bytes=VMEM
        ),
    )(flow, heat, salt)
    return pl.pallas_call(
        store,
        out_shape=tuple(jax.ShapeDtypeStruct(a.shape, f32) for a in (flow, heat, salt)),
        in_specs=[hbm] * 3,
        out_specs=(hbm,) * 3,
        scratch_shapes=[dma((6,))],
        compiler_params=pltpu.CompilerParams(vmem_limit_bytes=VMEM),
    )(vel, temp, out)


def solution(mesh):
    in_specs = (P(None, "gz", "gy", "gx"), P("gz", "gy", "gx"), P("gz", ("gx", "gy"), None))
    out_specs = (P(None, "gz", "gy", "gx"), P("gz", "gy", "gx"), P("gz", ("gx", "gy"), None))
    return jax.shard_map(
        functools.partial(on_device, mesh.shape["gx"], mesh.shape["gy"]),
        mesh=mesh, in_specs=in_specs, out_specs=out_specs, check_vma=False,
    )
```

```python
import functools

import jax
import jax.numpy as jnp
from jax import lax
from jax.experimental import pallas as pl
from jax.experimental.pallas import tpu as pltpu
from jax.sharding import PartitionSpec as P

time_step = 0.1
viscosity = 0.2
heat_diffusion = 0.15
salt_diffusion = 0.05
expansion = 1.0
thermal_expansion_curve = 0.5
contraction = 0.8
even_weights = (-0.0390625, 0.2734375, 0.8203125, -0.0546875)
odd_weights = (-0.0546875, 0.8203125, 0.2734375, -0.0390625)
diffusion = (viscosity, viscosity, viscosity, heat_diffusion)
VMEM = 64 * 1024 * 1024
OFF = 8
WIDE = 4


def split_dot(value, matrix, dims, count=3):
    rows = value.shape[0]
    parts = []
    for k in range(count):
        parts.append(value.astype(jnp.bfloat16))
        if k < count - 1:
            value = value - parts[-1].astype(jnp.float32)
    stacked = jnp.concatenate(parts, axis=0)
    out = lax.dot_general(stacked, matrix, (dims, ((), ())), preferred_element_type=jnp.float32)
    total = out[(count - 1) * rows :]
    for k in range(count - 2, -1, -1):
        total = out[k * rows : (k + 1) * rows] + total
    return total


def taps(weights, values):
    total = weights[0] * values[0]
    for weight, value in zip(weights[1:], values[1:]):
        total = total + weight * value
    return total


def advect(speed, centre, below, above):
    return jnp.maximum(speed, 0.0) * (centre - below) + jnp.minimum(speed, 0.0) * (above - centre)


def kernel(
    ngx, n, nr, nc, cx, ny,
    flow_in, heat_in, salt_in, vel_out, heat_out, salt_out,
    flow, heat, salt, turned, message, edge, got, got_edge, fields, mids, tall, fine,
    grains, grains_mid, mean_salt, results, outgoing, landed, fold, widen,
    main_send, main_recv, pass_send, edge_send, edge_recv, mean_send, mean_recv,
    rim_send, rim_recv, end_send, end_recv, load,
):
    gx, gy, gz = lax.axis_index("gx"), lax.axis_index("gy"), lax.axis_index("gz")
    other = 1 - gz
    r = gx * n + gy
    last = ngx * n - 1
    frame = nr + 2 * WIDE
    padded = nr + 2 * OFF
    f32 = jnp.float32

    def at(x, y, z):
        return {"gx": x, "gy": y, "gz": z}

    up_x, up_y = jnp.where(gy == n - 1, gx + 1, gx), jnp.where(gy == n - 1, 0, gy + 1)
    dn_x, dn_y = jnp.where(gy == 0, gx - 1, gx), jnp.where(gy == 0, n - 1, gy - 1)

    loads = [pltpu.make_async_copy(flow_in, flow, load.at[0]), pltpu.make_async_copy(heat_in, heat, load.at[1])]
    for c in range(nc // 64):
        loads.append(
            pltpu.make_async_copy(salt_in.at[:, :, 128 * c : 128 * (c + 1)], salt.at[:, c], load.at[2 + c])
        )
    for copy in loads:
        copy.start()

    barrier = pltpu.get_barrier_semaphore()

    def greet(x, y, z):
        pl.semaphore_signal(barrier, inc=1, device_id=at(x, y, z), device_id_type=pl.DeviceIdType.MESH)

    for d in range(1, n):
        greet(gx, lax.rem(gy + d, n), gz)
    greet(gx, gy, other)

    @pl.when(r > 0)
    def _():
        greet(dn_x, dn_y, gz)
        greet(dn_x, dn_y, other)

    @pl.when(r < last)
    def _():
        greet(up_x, up_y, gz)
        greet(up_x, up_y, other)

    takes_low = jnp.logical_and(gy == 0, gx > 0)
    takes_high = jnp.logical_and(gy == n - 1, gx < ngx - 1)

    @pl.when(takes_low)
    def _():
        for j in range(n):
            for z in range(2):
                greet(gx - 1, j, z)

    @pl.when(takes_high)
    def _():
        for j in range(n):
            for z in range(2):
                greet(gx + 1, j, z)

    loads[0].wait()
    loads[1].wait()
    tile = jnp.concatenate([flow[...].reshape(6 * cx, ny), heat[...].reshape(2 * cx, ny)], axis=0)
    lanes = 8 * cx
    zero8 = jnp.zeros((8, lanes), f32)
    turned[0:8] = zero8
    turned[8 + ny : 16 + ny] = zero8
    turned[8 : 8 + ny] = tile.T
    for j in range(n):
        base = 8 + nr * j
        message[j, 0:nr] = turned[base : base + nr]
        message[j, nr : nr + 4] = turned[base + nr : base + nr + 4]
        message[j, nr + 4 : nr + 8] = turned[base - 4 : base]
    edge[0, 0:4] = zero8[:4]
    edge[0, 4:8] = turned[4 + ny : 8 + ny]
    edge[1, 0:4] = turned[8:12]
    edge[1, 4:8] = zero8[:4]

    lowers = jnp.where(gx > 0, 2, 0)
    highers = jnp.where(gx < ngx - 1, 2, 0)
    sides = jnp.where(r > 0, 2, 0) + jnp.where(r < last, 2, 0)
    pl.semaphore_wait(barrier, n + sides + lowers + highers)

    def remote(src, dst, send, recv, x, y, z):
        return pltpu.make_async_remote_copy(
            src_ref=src, dst_ref=dst, send_sem=send, recv_sem=recv,
            device_id=at(x, y, z), device_id_type=pl.DeviceIdType.MESH,
        )

    def main(d):
        to = lax.rem(gy + d, n)
        return remote(message.at[to], got.at[gz, gy], main_send.at[d], main_recv.at[gz, gy], gx, to, gz)

    @pl.loop(1, n)
    def _(d):
        main(d).start()

    def passed(j, z):
        return remote(got.at[z, j], got.at[z, j], pass_send.at[j], main_recv.at[z, j], gx, gy, other)

    got[gz, gy] = message[gy]
    passed(gy, gz).start()

    def edge_copy(which, z):
        x = gx + 1 if which == 0 else gx - 1
        y = 0 if which == 0 else n - 1
        return remote(edge.at[which], got_edge.at[gz, gy], edge_send.at[which, z], edge_recv.at[gz, gy], x, y, z)

    @pl.when(gx < ngx - 1)
    def _():
        for z in range(2):
            edge_copy(0, z).start()

    @pl.when(gx > 0)
    def _():
        for z in range(2):
            edge_copy(1, z).start()

    takes_edge = jnp.logical_or(takes_low, takes_high)

    @pl.when(jnp.logical_not(takes_edge))
    def _():
        got_edge[...] = jnp.zeros(got_edge.shape, f32)

    row_id = lax.broadcasted_iota(jnp.int32, (2 * nc, 2 * nc), 0)
    col_id = lax.broadcasted_iota(jnp.int32, (2 * nc, 2 * nc), 1)
    source = jnp.where(col_id < nc, 2 * col_id, 2 * (col_id - nc) + 1)
    fold[...] = jnp.where(row_id == source, 1.0, 0.0).astype(jnp.bfloat16)
    for copy in loads[2:]:
        copy.wait()
    parts = []
    for lf in range(4):
        for rp in range(2):
            parts.append(
                jnp.concatenate(
                    [salt[lf, c, pl.ds(rp, nr, stride=2), :] for c in range(nc // 64)], axis=1
                )
            )
    folded = split_dot(jnp.concatenate(parts, axis=0), fold[...], ((1,), (0,)))
    for lf in range(4):
        for rp in range(2):
            k = (lf * 2 + rp) * nr
            grains[lf + 1, rp, OFF : OFF + nr] = folded[k : k + nr]

    def walls(buf):
        @pl.when(gz == 0)
        def _():
            buf[0] = jnp.zeros(buf.shape[1:], f32)

        @pl.when(gz == 1)
        def _():
            buf[5] = jnp.zeros(buf.shape[1:], f32)

        @pl.when(r == 0)
        def _():
            buf[1:5, 1, 0:OFF] = jnp.zeros((4, OFF, 2 * nc), f32)

        @pl.when(r == last)
        def _():
            buf[1:5, 0, OFF + nr : padded] = jnp.zeros((4, OFF, 2 * nc), f32)

    own = pl.ds(OFF, nr)

    def rims(buf, s):
        down = remote(
            buf.at[1:5, 0, OFF : OFF + 8], buf.at[1:5, 0, OFF + nr : padded],
            rim_send.at[s, 1], rim_recv.at[s, 1], dn_x, dn_y, gz,
        )
        up = remote(
            buf.at[1:5, 1, nr : OFF + nr], buf.at[1:5, 1, 0:OFF],
            rim_send.at[s, 2], rim_recv.at[s, 2], up_x, up_y, gz,
        )
        return down, up

    def rim_start(buf, s):
        down, up = rims(buf, s)
        level_copy(buf, s).start()

        @pl.when(r > 0)
        def _():
            down.start()

        @pl.when(r < last)
        def _():
            up.start()

    def level_copy(buf, s):
        return remote(
            buf.at[4 - 3 * gz, :, own], buf.at[5 * gz, :, own], rim_send.at[s, 0], rim_recv.at[s, 0], gx, gy, other
        )

    def level_landed(buf, s):
        return remote(
            buf.at[4 - 3 * gz, :, own], buf.at[5 * (1 - gz), :, own], rim_send.at[s, 0], rim_recv.at[s, 0], gx, gy, other
        )

    def rim_wait(buf, s):
        down, up = rims(buf, s)
        level_landed(buf, s).wait_recv()
        level_copy(buf, s).wait_send()

        @pl.when(r > 0)
        def _():
            up.wait_recv()
            down.wait_send()

        @pl.when(r < last)
        def _():
            down.wait_recv()
            up.wait_send()

    walls(grains)
    rim_start(grains, 0)

    def halves(value):
        return value[:, :nc] + value[:, nc:]

    for l in range(2):
        total = sum(grains[1 + 2 * l + p, q, OFF : OFF + nr] for p in range(2) for q in range(2))
        mean_salt[gz * 2 + l, OFF : OFF + nr] = 0.125 * halves(total)

    @pl.when(r == 0)
    def _():
        mean_salt[:, 0:OFF] = jnp.zeros((4, OFF, nc), f32)

    @pl.when(r == last)
    def _():
        mean_salt[:, OFF + nr : padded] = jnp.zeros((4, OFF, nc), f32)

    def mean_copy(k):
        mine = pl.ds(gz * 2, 2)
        if k == 0:
            part = mean_salt.at[mine, OFF : OFF + nr]
            return remote(part, part, mean_send.at[0], mean_recv.at[0], gx, gy, other)
        z = gz if k % 2 else other
        if k < 3:
            return remote(
                mean_salt.at[mine, nr : OFF + nr], mean_salt.at[mine, 0:OFF],
                mean_send.at[k], mean_recv.at[k], up_x, up_y, z,
            )
        return remote(
            mean_salt.at[mine, OFF : OFF + 8], mean_salt.at[mine, OFF + nr : padded],
            mean_send.at[k], mean_recv.at[k], dn_x, dn_y, z,
        )

    def mean_landed(k):
        from_z = gz if k % 2 else other
        theirs = pl.ds(from_z * 2, 2)
        if k == 0:
            part = mean_salt.at[theirs, OFF : OFF + nr]
        elif k < 3:
            part = mean_salt.at[theirs, 0:OFF]
        else:
            part = mean_salt.at[theirs, OFF + nr : padded]
        return remote(part, part, mean_send.at[k], mean_recv.at[k], gx, gy, other)

    mean_copy(0).start()

    @pl.when(r < last)
    def _():
        mean_copy(1).start()
        mean_copy(2).start()

    @pl.when(r > 0)
    def _():
        mean_copy(3).start()
        mean_copy(4).start()

    @pl.loop(1, n)
    def _(d):
        j = lax.rem(gy + n - d, n)
        passed(j, gz).wait_recv()
        passed(j, gz).start()

    row_id = lax.broadcasted_iota(jnp.int32, (nc, 2 * nc), 0)
    col_id = lax.broadcasted_iota(jnp.int32, (nc, 2 * nc), 1)
    odd = col_id >= nc
    step = row_id - jnp.where(odd, col_id - nc - 1, col_id - 2)
    band = jnp.zeros((nc, 2 * nc), f32)
    for k in range(4):
        band = jnp.where(step == k, jnp.where(odd, odd_weights[k], even_weights[k]), band)
    widen[...] = band.astype(jnp.bfloat16)

    for f in range(4):
        for level in (0, 1, 6, 7):
            tall[f, level] = jnp.zeros((2, frame, nc), f32)
    for f in range(4):
        for level in (0, 5):
            fields[f, level] = jnp.zeros((padded, nc), f32)
            mids[f, level] = jnp.zeros((padded, nc), f32)

    @pl.when(takes_edge)
    def _():
        for z in range(2):
            for j in range(n):
                remote(edge.at[0], got_edge.at[z, j], edge_send.at[0, 0], edge_recv.at[z, j], gx, gy, other).wait_recv()

    chunk = lax.broadcasted_iota(jnp.int32, (nr + 8, 128), 1) // cx
    per = 128 // cx

    def gather_chunks(values, k):
        out = None
        for j, value in enumerate(values):
            shift = (cx * (j - k)) % 128
            moved = pltpu.roll(value, shift, axis=1) if shift else value
            out = moved if out is None else jnp.where(chunk[: value.shape[0]] == j, moved, out)
        return out

    def assemble(z):
        @pl.loop(0, (lanes // 128) * (n // per))
        def _(i):
            t, a = i // (n // per), lax.rem(i, n // per)
            part = pl.ds(pl.multiple_of(128 * t, 128), 128)
            where = pl.ds(pl.multiple_of(128 * a, 128), 128)
            values = []
            for j in range(per):
                body = got[z, per * a + j, 0:nr, part]
                rim = got[z, per * a + j, nr : nr + 8, part] + got_edge[z, per * a + j, :, part]
                values.append(jnp.concatenate([body, rim], axis=0))
            for k in range(per):
                whole = gather_chunks(values, k)
                f, level = (per // 2) * t + k // 2, z * 2 + k % 2 + 1
                fields[f, level, OFF : OFF + nr, where] = whole[:nr]
                fields[f, level, 0:8, where] = whole[nr:]
                fields[f, level, OFF + nr : padded, where] = whole[nr:]

    lo = OFF - WIDE

    def row_taps(buf, f, level, start, count, rp):
        weights = (even_weights, odd_weights)[rp]
        base = start - 2 + rp
        return taps(weights, [buf[f, level, base + k : base + k + count] for k in range(4)])

    def refine_rows(buf, z, start, count):
        @pl.loop(0, 6)
        def _(i):
            f, level = i // 2, z * 2 + lax.rem(i, 2)
            for rp in range(2):
                tall[f, level + 2, rp, 0:nr] = row_taps(buf, f, level + 1, OFF, nr, rp)

        @pl.loop(0, 2)
        def _(l):
            level = z * 2 + l
            for rp in range(2):
                tall[3, level + 2, rp, 0:count] = row_taps(buf, 3, level + 1, start, count, rp)

    assemble(gz)
    refine_rows(fields, gz, lo, frame)
    @pl.loop(0, n)
    def _(d):
        passed(lax.rem(gy + d, n), other).wait_recv()

    assemble(other)
    refine_rows(fields, other, lo, frame)

    def level_taps(f, first, p, count):
        values = [tall[f, first + k + p, :, 0:count].reshape(2 * count, nc) for k in range(4)]
        return taps((even_weights, odd_weights)[p], values)

    def widen_pairs(f, firsts, count):
        parts = [level_taps(f, first, p, count) for first in firsts for p in range(2)]
        return split_dot(jnp.concatenate(parts, axis=0), widen[...], ((1,), (0,)), 2)

    def refine_speeds():
        @pl.loop(0, 3)
        def _(f):
            out = widen_pairs(f, (2 * gz, 2 * gz + 1), nr)
            for k in range(8):
                fine[f, k // 2, k % 2] = out[k * nr : (k + 1) * nr]

    def warm_mean(level, count):
        x = widen_pairs(3, (level,), count)
        x = expansion * x * (1.0 + thermal_expansion_curve * x)
        return 0.125 * halves(
            (x[:count] + x[count : 2 * count]) + (x[2 * count : 3 * count] + x[3 * count :])
        )

    refine_speeds()
    rim_wait(grains, 0)
    lane = lax.broadcasted_iota(jnp.int32, (nr, nc), 1)

    def salt_rate(buf, lf, rp):
        centre = buf[lf + 1, rp, OFF : OFF + nr]
        lower, upper = buf[lf, rp, OFF : OFF + nr], buf[lf + 2, rp, OFF : OFF + nr]
        if rp == 0:
            before, after = buf[lf + 1, 1, OFF - 1 : OFF - 1 + nr], buf[lf + 1, 1, OFF : OFF + nr]
        else:
            before, after = buf[lf + 1, 0, OFF : OFF + nr], buf[lf + 1, 0, OFF + 1 : OFF + 1 + nr]
        even, uneven = centre[:, :nc], centre[:, nc:]
        left = jnp.concatenate([jnp.where(lane == 0, 0.0, pltpu.roll(uneven, 1, axis=1)), even], axis=1)
        right = jnp.concatenate([uneven, jnp.where(lane == nc - 1, 0.0, pltpu.roll(even, nc - 1, axis=1))], axis=1)
        w, u, v = [fine[f, lf, rp] for f in range(3)]
        flux = advect(w, centre, lower, upper) + advect(v, centre, before, after) + advect(u, centre, left, right)
        around = (lower + upper) + (before + after) + (left + right)
        return centre, (4.0 * salt_diffusion) * (around - 6.0 * centre) - 2.0 * flux

    @pl.loop(0, 4)
    def _(lf):
        for rp in range(2):
            centre, rate = salt_rate(grains, lf, rp)
            grains_mid[lf + 1, rp, OFF : OFF + nr] = centre + time_step * rate

    walls(grains_mid)
    rim_start(grains_mid, 1)

    mean_landed(0).wait_recv()

    @pl.when(r > 0)
    def _():
        mean_landed(1).wait_recv()
        mean_landed(2).wait_recv()

    @pl.when(r < last)
    def _():
        mean_landed(3).wait_recv()
        mean_landed(4).wait_recv()

    def coarse_step(buf, level, start, count, lift):
        here = lax.broadcasted_iota(jnp.int32, (count, nc), 1)
        rows = pl.ds(start, count)
        centres = [buf[f, level, rows] for f in range(4)]
        out = []
        for f in range(4):
            q = centres[f]
            lower, upper = buf[f, level - 1, rows], buf[f, level + 1, rows]
            before, after = buf[f, level, start - 1 : start - 1 + count], buf[f, level, start + 1 : start + 1 + count]
            left = jnp.where(here == 0, 0.0, pltpu.roll(q, 1, axis=1))
            right = jnp.where(here == nc - 1, 0.0, pltpu.roll(q, nc - 1, axis=1))
            flux = (
                advect(centres[0], q, lower, upper)
                + advect(centres[1], q, left, right)
                + advect(centres[2], q, before, after)
            )
            around = (lower + upper) + (before + after) + (left + right)
            rate = diffusion[f] * (around - 6.0 * q) - flux
            out.append((q, rate + lift if f == 0 else rate))
        return out

    row = lax.broadcasted_iota(jnp.int32, (frame, nc), 0) + (r * nr - WIDE)
    inside = jnp.logical_and(row >= 0, row < (last + 1) * nr)
    for f in range(4):
        for level in range(4):
            mids[f, level + 1, 0:8] = jnp.zeros((8, nc), f32)
            mids[f, level + 1, OFF + nr : padded] = jnp.zeros((8, nc), f32)

    @pl.loop(0, 4)
    def _(level):
        lift = warm_mean(level, frame) - contraction * mean_salt[level, lo : lo + frame]
        for f, (q, rate) in enumerate(coarse_step(fields, level + 1, lo, frame, lift)):
            mids[f, level + 1, lo : lo + frame] = jnp.where(inside, q + time_step * rate, 0.0)

    for z in range(2):
        refine_rows(mids, z, OFF, nr)

    @pl.loop(0, 2)
    def _(l):
        salts = sum(grains_mid[1 + 2 * l + p, q, OFF : OFF + nr] for p in range(2) for q in range(2))
        level = gz * 2 + l
        lift = warm_mean(level, nr) - (0.125 * contraction) * halves(salts)
        for f, (q, rate) in enumerate(coarse_step(mids, level + 1, OFF, nr, lift)):
            results[2 * f + l] = 0.5 * fields[f, level + 1, OFF : OFF + nr] + 0.5 * (q + time_step * rate)

    @pl.loop(0, (lanes // 128) * (n // per))
    def _(i):
        t, a = i // (n // per), lax.rem(i, n // per)
        part = pl.ds(pl.multiple_of(128 * t, 128), 128)
        where = pl.ds(pl.multiple_of(128 * a, 128), 128)
        values = [results[per * t + k, :, where] for k in range(per)]
        for j in range(per):
            outgoing[per * a + j, :, part] = gather_chunks(values, j)

    def end(d):
        to = lax.rem(gy + d, n)
        return remote(outgoing.at[to], landed.at[gy], end_send.at[d], end_recv.at[gy], gx, to, gz)

    @pl.loop(1, n)
    def _(d):
        end(d).start()

    landed[gy] = outgoing[gy]

    refine_speeds()
    rim_wait(grains_mid, 1)

    @pl.loop(0, 4)
    def _(lf):
        for rp in range(2):
            centre, rate = salt_rate(grains_mid, lf, rp)
            grains[lf + 1, rp, OFF : OFF + nr] = 0.5 * grains[lf + 1, rp, OFF : OFF + nr] + 0.5 * (
                centre + time_step * rate
            )

    parts = [grains[lf + 1, rp, OFF : OFF + nr] for lf in range(4) for rp in range(2)]
    whole = split_dot(jnp.concatenate(parts, axis=0), fold[...], ((1,), (1,)))
    for lf in range(4):
        for rp in range(2):
            k = (lf * 2 + rp) * nr
            for c in range(nc // 64):
                salt[lf, c, pl.ds(rp, nr, stride=2), :] = whole[k : k + nr, 128 * c : 128 * (c + 1)]

    stores = [
        pltpu.make_async_copy(salt.at[:, c], salt_out.at[:, :, 128 * c : 128 * (c + 1)], load.at[2 + c])
        for c in range(nc // 64)
    ]
    for copy in stores:
        copy.start()

    @pl.loop(1, n)
    def _(d):
        j = lax.rem(gy + n - d, n)
        remote(outgoing.at[j], landed.at[j], end_send.at[d], end_recv.at[j], gx, j, gz).wait_recv()

    back = landed[...].reshape(ny, lanes).T
    flow[...] = back[: 6 * cx].reshape(3, 2, cx, ny)
    heat[...] = back[6 * cx :].reshape(2, cx, ny)
    stores += [pltpu.make_async_copy(flow, vel_out, load.at[0]), pltpu.make_async_copy(heat, heat_out, load.at[1])]
    for copy in stores[-2:]:
        copy.start()

    @pl.loop(1, n)
    def _(d):
        main(d).wait_send()
        end(d).wait_send()

    @pl.loop(0, n)
    def _(j):
        passed(j, gz).wait_send()

    mean_copy(0).wait_send()

    @pl.when(gx < ngx - 1)
    def _():
        for z in range(2):
            edge_copy(0, z).wait_send()

    @pl.when(gx > 0)
    def _():
        for z in range(2):
            edge_copy(1, z).wait_send()

    @pl.when(r < last)
    def _():
        mean_copy(1).wait_send()
        mean_copy(2).wait_send()

    @pl.when(r > 0)
    def _():
        mean_copy(3).wait_send()
        mean_copy(4).wait_send()

    for copy in stores:
        copy.wait()


def store(*refs):
    ins, outs, held, sems = refs[:3], refs[3:6], refs[6:9], refs[9]
    pairs = []
    for k in range(3):
        for i in range(ins[k].shape[0]):
            sem = sems.at[k, i]
            pairs.append(
                (
                    pltpu.make_async_copy(ins[k].at[i], held[k].at[i], sem),
                    pltpu.make_async_copy(held[k].at[i], outs[k].at[i], sem),
                )
            )
    for first, _ in pairs:
        first.start()
    for first, second in pairs:
        first.wait()
        second.start()
    for _, second in pairs:
        second.wait()


def on_device(ngx, n, flow, heat, salt):
    cx, ny = flow.shape[2], flow.shape[3]
    nr, nc = salt.shape[1] // 2, salt.shape[2] // 2
    padded = nr + 2 * OFF
    lanes = 8 * cx
    f32, dma = jnp.float32, pltpu.SemaphoreType.DMA
    hbm = pl.BlockSpec(memory_space=pltpu.HBM)
    vel, temp, out = pl.pallas_call(
        functools.partial(kernel, ngx, n, nr, nc, cx, ny),
        out_shape=(
            jax.ShapeDtypeStruct(flow.shape, f32),
            jax.ShapeDtypeStruct(heat.shape, f32),
            jax.ShapeDtypeStruct(salt.shape, f32),
        ),
        in_specs=[hbm] * 3,
        out_specs=(hbm,) * 3,
        scratch_shapes=[
            pltpu.VMEM(flow.shape, f32),
            pltpu.VMEM(heat.shape, f32),
            pltpu.VMEM((4, nc // 64, 2 * nr, 128), f32),
            pltpu.VMEM((ny + 16, lanes), f32),
            pltpu.VMEM((n, nr + 8, lanes), f32),
            pltpu.VMEM((2, 8, lanes), f32),
            pltpu.VMEM((2, n, nr + 8, lanes), f32),
            pltpu.VMEM((2, n, 8, lanes), f32),
            pltpu.VMEM((4, 6, padded, nc), f32),
            pltpu.VMEM((4, 6, padded, nc), f32),
            pltpu.VMEM((4, 8, 2, nr + 2 * WIDE, nc), f32),
            pltpu.VMEM((3, 4, 2, nr, 2 * nc), f32),
            pltpu.VMEM((6, 2, padded, 2 * nc), f32),
            pltpu.VMEM((6, 2, padded, 2 * nc), f32),
            pltpu.VMEM((4, padded, nc), f32),
            pltpu.VMEM((8, nr, nc), f32),
            pltpu.VMEM((n, nr, lanes), f32),
            pltpu.VMEM((n, nr, lanes), f32),
            pltpu.VMEM((2 * nc, 2 * nc), jnp.bfloat16),
            pltpu.VMEM((nc, 2 * nc), jnp.bfloat16),
            dma((n,)), dma((2, n)), dma((n,)), dma((2, 2)), dma((2, n)), dma((5,)), dma((5,)),
            dma((2, 3)), dma((2, 3)), dma((n,)), dma((n,)), dma((2 + nc // 64,)),
        ],
        compiler_params=pltpu.CompilerParams(
            collective_id=0, has_side_effects=True, vmem_limit_bytes=VMEM
        ),
    )(flow, heat, salt)
    return pl.pallas_call(
        store,
        out_shape=tuple(jax.ShapeDtypeStruct(a.shape, f32) for a in (flow, heat, salt)),
        in_specs=[hbm] * 3,
        out_specs=(hbm,) * 3,
        scratch_shapes=[pltpu.VMEM(a.shape, f32) for a in (flow, heat, salt)] + [dma((3, 4))],
        compiler_params=pltpu.CompilerParams(vmem_limit_bytes=VMEM),
    )(vel, temp, out)


def solution(mesh):
    in_specs = (P(None, "gz", "gy", "gx"), P("gz", "gy", "gx"), P("gz", ("gx", "gy"), None))
    out_specs = (P(None, "gz", "gy", "gx"), P("gz", "gy", "gx"), P("gz", ("gx", "gy"), None))
    return jax.shard_map(
        functools.partial(on_device, mesh.shape["gx"], mesh.shape["gy"]),
        mesh=mesh, in_specs=in_specs, out_specs=out_specs, check_vma=False,
    )
```

```python
import functools

import jax
import jax.numpy as jnp
from jax import lax
from jax.experimental import pallas as pl
from jax.experimental.pallas import tpu as pltpu
from jax.sharding import PartitionSpec as P

time_step = 0.1
viscosity = 0.2
heat_diffusion = 0.15
salt_diffusion = 0.05
expansion = 1.0
thermal_expansion_curve = 0.5
contraction = 0.8
even_weights = (-0.0390625, 0.2734375, 0.8203125, -0.0546875)
odd_weights = (-0.0546875, 0.8203125, 0.2734375, -0.0390625)
diffusion = (viscosity, viscosity, viscosity, heat_diffusion)
VMEM = 64 * 1024 * 1024
OFF = 8
WIDE = 4


def split_dot(value, matrix, dims, count=3):
    rows = value.shape[0]
    parts = []
    for k in range(count):
        parts.append(value.astype(jnp.bfloat16))
        if k < count - 1:
            value = value - parts[-1].astype(jnp.float32)
    stacked = jnp.concatenate(parts, axis=0)
    out = lax.dot_general(stacked, matrix, (dims, ((), ())), preferred_element_type=jnp.float32)
    total = out[(count - 1) * rows :]
    for k in range(count - 2, -1, -1):
        total = out[k * rows : (k + 1) * rows] + total
    return total


def taps(weights, values):
    total = weights[0] * values[0]
    for weight, value in zip(weights[1:], values[1:]):
        total = total + weight * value
    return total


def advect(speed, centre, below, above):
    return jnp.maximum(speed, 0.0) * (centre - below) + jnp.minimum(speed, 0.0) * (above - centre)


def kernel(
    ngx, n, nr, nc, cx, ny,
    flow_in, heat_in, salt_in, vel_out, heat_out, salt_out,
    flow, heat, salt, turned, message, edge, got, got_edge, fields, mids, tall, fine,
    grains, grains_mid, mean_salt, buoy, outgoing, landed, fold, widen,
    main_send, main_recv, pass_send, edge_send, edge_recv, mean_send, mean_recv,
    rim_send, rim_recv, end_send, end_recv, load,
):
    gx, gy, gz = lax.axis_index("gx"), lax.axis_index("gy"), lax.axis_index("gz")
    other = 1 - gz
    r = gx * n + gy
    last = ngx * n - 1
    frame = nr + 2 * WIDE
    padded = nr + 2 * OFF
    f32 = jnp.float32

    def at(x, y, z):
        return {"gx": x, "gy": y, "gz": z}

    up_x, up_y = jnp.where(gy == n - 1, gx + 1, gx), jnp.where(gy == n - 1, 0, gy + 1)
    dn_x, dn_y = jnp.where(gy == 0, gx - 1, gx), jnp.where(gy == 0, n - 1, gy - 1)

    loads = [pltpu.make_async_copy(flow_in, flow, load.at[0]), pltpu.make_async_copy(heat_in, heat, load.at[1])]
    for c in range(nc // 64):
        loads.append(
            pltpu.make_async_copy(salt_in.at[:, :, 128 * c : 128 * (c + 1)], salt.at[:, c], load.at[2 + c])
        )
    for copy in loads:
        copy.start()

    barrier = pltpu.get_barrier_semaphore()

    def greet(x, y, z):
        pl.semaphore_signal(barrier, inc=1, device_id=at(x, y, z), device_id_type=pl.DeviceIdType.MESH)

    for d in range(1, n):
        greet(gx, lax.rem(gy + d, n), gz)
    greet(gx, gy, other)

    @pl.when(r > 0)
    def _():
        greet(dn_x, dn_y, gz)
        greet(dn_x, dn_y, other)

    @pl.when(r < last)
    def _():
        greet(up_x, up_y, gz)
        greet(up_x, up_y, other)

    takes_low = jnp.logical_and(gy == 0, gx > 0)
    takes_high = jnp.logical_and(gy == n - 1, gx < ngx - 1)

    @pl.when(takes_low)
    def _():
        for j in range(n):
            for z in range(2):
                greet(gx - 1, j, z)

    @pl.when(takes_high)
    def _():
        for j in range(n):
            for z in range(2):
                greet(gx + 1, j, z)

    loads[0].wait()
    loads[1].wait()
    tile = jnp.concatenate([flow[...].reshape(6 * cx, ny), heat[...].reshape(2 * cx, ny)], axis=0)
    lanes = 8 * cx
    zero8 = jnp.zeros((8, lanes), f32)
    turned[0:8] = zero8
    turned[8 + ny : 16 + ny] = zero8
    turned[8 : 8 + ny] = tile.T
    for j in range(n):
        base = 8 + nr * j
        message[j, 0:nr] = turned[base : base + nr]
        message[j, nr : nr + 4] = turned[base + nr : base + nr + 4]
        message[j, nr + 4 : nr + 8] = turned[base - 4 : base]
    edge[0, 0:4] = zero8[:4]
    edge[0, 4:8] = turned[4 + ny : 8 + ny]
    edge[1, 0:4] = turned[8:12]
    edge[1, 4:8] = zero8[:4]

    lowers = jnp.where(gx > 0, 2, 0)
    highers = jnp.where(gx < ngx - 1, 2, 0)
    sides = jnp.where(r > 0, 2, 0) + jnp.where(r < last, 2, 0)
    pl.semaphore_wait(barrier, n + sides + lowers + highers)

    def remote(src, dst, send, recv, x, y, z):
        return pltpu.make_async_remote_copy(
            src_ref=src, dst_ref=dst, send_sem=send, recv_sem=recv,
            device_id=at(x, y, z), device_id_type=pl.DeviceIdType.MESH,
        )

    main = []
    for d in range(1, n):
        to = lax.rem(gy + d, n)
        main.append(remote(message.at[to], got.at[gz, gy], main_send.at[d], main_recv.at[gz, gy], gx, to, gz))
        main[-1].start()

    def passed(j, z):
        return remote(got.at[z, j], got.at[z, j], pass_send.at[j], main_recv.at[z, j], gx, gy, other)

    got[gz, gy] = message[gy]
    passed(gy, gz).start()

    def edge_copy(which, z):
        x = gx + 1 if which == 0 else gx - 1
        y = 0 if which == 0 else n - 1
        return remote(edge.at[which], got_edge.at[gz, gy], edge_send.at[which, z], edge_recv.at[gz, gy], x, y, z)

    @pl.when(gx < ngx - 1)
    def _():
        for z in range(2):
            edge_copy(0, z).start()

    @pl.when(gx > 0)
    def _():
        for z in range(2):
            edge_copy(1, z).start()

    takes_edge = jnp.logical_or(takes_low, takes_high)

    @pl.when(jnp.logical_not(takes_edge))
    def _():
        got_edge[...] = jnp.zeros(got_edge.shape, f32)

    row_id = lax.broadcasted_iota(jnp.int32, (2 * nc, 2 * nc), 0)
    col_id = lax.broadcasted_iota(jnp.int32, (2 * nc, 2 * nc), 1)
    source = jnp.where(col_id < nc, 2 * col_id, 2 * (col_id - nc) + 1)
    fold[...] = jnp.where(row_id == source, 1.0, 0.0).astype(jnp.bfloat16)
    for copy in loads[2:]:
        copy.wait()
    parts = []
    for lf in range(4):
        for rp in range(2):
            parts.append(
                jnp.concatenate(
                    [salt[lf, c, pl.ds(rp, nr, stride=2), :] for c in range(nc // 64)], axis=1
                )
            )
    folded = split_dot(jnp.concatenate(parts, axis=0), fold[...], ((1,), (0,)))
    for lf in range(4):
        for rp in range(2):
            k = (lf * 2 + rp) * nr
            grains[lf + 1, rp, OFF : OFF + nr] = folded[k : k + nr]

    def walls(buf):
        @pl.when(gz == 0)
        def _():
            buf[0] = jnp.zeros(buf.shape[1:], f32)

        @pl.when(gz == 1)
        def _():
            buf[5] = jnp.zeros(buf.shape[1:], f32)

        @pl.when(r == 0)
        def _():
            buf[1:5, 1, 0:OFF] = jnp.zeros((4, OFF, 2 * nc), f32)

        @pl.when(r == last)
        def _():
            buf[1:5, 0, OFF + nr : padded] = jnp.zeros((4, OFF, 2 * nc), f32)

    own = pl.ds(OFF, nr)

    def rims(buf, s):
        down = remote(
            buf.at[1:5, 0, OFF : OFF + 8], buf.at[1:5, 0, OFF + nr : padded],
            rim_send.at[s, 1], rim_recv.at[s, 1], dn_x, dn_y, gz,
        )
        up = remote(
            buf.at[1:5, 1, nr : OFF + nr], buf.at[1:5, 1, 0:OFF],
            rim_send.at[s, 2], rim_recv.at[s, 2], up_x, up_y, gz,
        )
        return down, up

    def rim_start(buf, s):
        down, up = rims(buf, s)
        level_copy(buf, s).start()

        @pl.when(r > 0)
        def _():
            down.start()

        @pl.when(r < last)
        def _():
            up.start()

    def level_copy(buf, s):
        return remote(
            buf.at[4 - 3 * gz, :, own], buf.at[5 * gz, :, own], rim_send.at[s, 0], rim_recv.at[s, 0], gx, gy, other
        )

    def level_landed(buf, s):
        return remote(
            buf.at[4 - 3 * gz, :, own], buf.at[5 * (1 - gz), :, own], rim_send.at[s, 0], rim_recv.at[s, 0], gx, gy, other
        )

    def rim_wait(buf, s):
        down, up = rims(buf, s)
        level_landed(buf, s).wait_recv()
        level_copy(buf, s).wait_send()

        @pl.when(r > 0)
        def _():
            up.wait_recv()
            down.wait_send()

        @pl.when(r < last)
        def _():
            down.wait_recv()
            up.wait_send()

    walls(grains)

    def halves(value):
        return value[:, :nc] + value[:, nc:]

    for l in range(2):
        total = sum(grains[1 + 2 * l + p, q, OFF : OFF + nr] for p in range(2) for q in range(2))
        mean_salt[gz * 2 + l, OFF : OFF + nr] = 0.125 * halves(total)

    @pl.when(r == 0)
    def _():
        mean_salt[:, 0:OFF] = jnp.zeros((4, OFF, nc), f32)

    @pl.when(r == last)
    def _():
        mean_salt[:, OFF + nr : padded] = jnp.zeros((4, OFF, nc), f32)

    def mean_copy(k):
        mine = pl.ds(gz * 2, 2)
        if k == 0:
            part = mean_salt.at[mine, OFF : OFF + nr]
            return remote(part, part, mean_send.at[0], mean_recv.at[0], gx, gy, other)
        z = gz if k % 2 else other
        if k < 3:
            return remote(
                mean_salt.at[mine, nr : OFF + nr], mean_salt.at[mine, 0:OFF],
                mean_send.at[k], mean_recv.at[k], up_x, up_y, z,
            )
        return remote(
            mean_salt.at[mine, OFF : OFF + 8], mean_salt.at[mine, OFF + nr : padded],
            mean_send.at[k], mean_recv.at[k], dn_x, dn_y, z,
        )

    def mean_landed(k):
        from_z = gz if k % 2 else other
        theirs = pl.ds(from_z * 2, 2)
        if k == 0:
            part = mean_salt.at[theirs, OFF : OFF + nr]
        elif k < 3:
            part = mean_salt.at[theirs, 0:OFF]
        else:
            part = mean_salt.at[theirs, OFF + nr : padded]
        return remote(part, part, mean_send.at[k], mean_recv.at[k], gx, gy, other)

    mean_copy(0).start()

    @pl.when(r < last)
    def _():
        mean_copy(1).start()
        mean_copy(2).start()

    @pl.when(r > 0)
    def _():
        mean_copy(3).start()
        mean_copy(4).start()

    for d in range(1, n):
        j = lax.rem(gy + n - d, n)
        passed(j, gz).wait_recv()
        passed(j, gz).start()
    rim_start(grains, 0)

    row_id = lax.broadcasted_iota(jnp.int32, (nc, 2 * nc), 0)
    col_id = lax.broadcasted_iota(jnp.int32, (nc, 2 * nc), 1)
    odd = col_id >= nc
    step = row_id - jnp.where(odd, col_id - nc - 1, col_id - 2)
    band = jnp.zeros((nc, 2 * nc), f32)
    for k in range(4):
        band = jnp.where(step == k, jnp.where(odd, odd_weights[k], even_weights[k]), band)
    widen[...] = band.astype(jnp.bfloat16)

    for f in range(4):
        for level in (0, 1, 6, 7):
            tall[f, level] = jnp.zeros((2, frame, nc), f32)
    for f in range(4):
        for level in (0, 5):
            fields[f, level] = jnp.zeros((padded, nc), f32)
            mids[f, level] = jnp.zeros((padded, nc), f32)

    @pl.when(takes_edge)
    def _():
        for z in range(2):
            for j in range(n):
                remote(edge.at[0], got_edge.at[z, j], edge_send.at[0, 0], edge_recv.at[z, j], gx, gy, other).wait_recv()

    chunk = lax.broadcasted_iota(jnp.int32, (nr + 8, 128), 1) // cx
    per = 128 // cx

    def gather_chunks(values, k):
        out = None
        for j, value in enumerate(values):
            shift = (cx * (j - k)) % 128
            moved = pltpu.roll(value, shift, axis=1) if shift else value
            out = moved if out is None else jnp.where(chunk[: value.shape[0]] == j, moved, out)
        return out

    def assemble(z):
        for t in range(lanes // 128):
            for a in range(n // per):
                values = []
                for j in range(per):
                    body = got[z, per * a + j, 0:nr, 128 * t : 128 * (t + 1)]
                    rim = (
                        got[z, per * a + j, nr : nr + 8, 128 * t : 128 * (t + 1)]
                        + got_edge[z, per * a + j, :, 128 * t : 128 * (t + 1)]
                    )
                    values.append(jnp.concatenate([body, rim], axis=0))
                for k in range(per):
                    pair = per * t + k
                    f, l = pair // 2, pair % 2
                    whole = gather_chunks(values, k)
                    where = slice(128 * a, 128 * (a + 1))
                    level = z * 2 + l + 1
                    fields[f, level, OFF : OFF + nr, where] = whole[:nr]
                    fields[f, level, 0:8, where] = whole[nr:]
                    fields[f, level, OFF + nr : padded, where] = whole[nr:]

    lo = OFF - WIDE

    def row_taps(buf, f, level, start, count, rp):
        weights = (even_weights, odd_weights)[rp]
        base = start - 2 + rp
        return taps(weights, [buf[f, level, base + k : base + k + count] for k in range(4)])

    def refine_rows(buf, z, start, count):
        for l in range(2):
            level = z * 2 + l
            for rp in range(2):
                for f in range(3):
                    tall[f, level + 2, rp, 0:nr] = row_taps(buf, f, level + 1, OFF, nr, rp)
                tall[3, level + 2, rp, 0:count] = row_taps(buf, 3, level + 1, start, count, rp)

    assemble(gz)
    refine_rows(fields, gz, lo, frame)
    for d in range(n):
        j = lax.rem(gy + d, n)
        passed(j, other).wait_recv()
    assemble(other)
    refine_rows(fields, other, lo, frame)

    def level_taps(f, base, lf, count):
        p = lf % 2
        values, weights = [], []
        for k in range(4):
            level = base + lf // 2 + k + p
            if isinstance(level, int) and not 2 <= level < 6:
                continue
            values.append(tall[f, level, :, 0:count].reshape(2 * count, nc))
            weights.append((even_weights, odd_weights)[p][k])
        return taps(weights, values)

    def widen_pair(f, base, lf, count):
        pair = jnp.concatenate([level_taps(f, base, lf, count), level_taps(f, base, lf + 1, count)], axis=0)
        return split_dot(pair, widen[...], ((1,), (0,)), 2)

    def refine_speeds():
        for f in range(3):
            for lf in (0, 2):
                out = widen_pair(f, 2 * gz, lf, nr)
                for k in range(4):
                    fine[f, lf + k // 2, k % 2] = out[k * nr : (k + 1) * nr]

    def warm_mean(base, l, count):
        x = widen_pair(3, base, 2 * l, count)
        x = expansion * x * (1.0 + thermal_expansion_curve * x)
        return 0.125 * halves(
            (x[:count] + x[count : 2 * count]) + (x[2 * count : 3 * count] + x[3 * count :])
        )

    refine_speeds()
    rim_wait(grains, 0)
    lane = lax.broadcasted_iota(jnp.int32, (nr, nc), 1)

    def salt_rate(buf, lf, rp):
        centre = buf[lf + 1, rp, OFF : OFF + nr]
        lower, upper = buf[lf, rp, OFF : OFF + nr], buf[lf + 2, rp, OFF : OFF + nr]
        if rp == 0:
            before, after = buf[lf + 1, 1, OFF - 1 : OFF - 1 + nr], buf[lf + 1, 1, OFF : OFF + nr]
        else:
            before, after = buf[lf + 1, 0, OFF : OFF + nr], buf[lf + 1, 0, OFF + 1 : OFF + 1 + nr]
        even, uneven = centre[:, :nc], centre[:, nc:]
        left = jnp.concatenate([jnp.where(lane == 0, 0.0, pltpu.roll(uneven, 1, axis=1)), even], axis=1)
        right = jnp.concatenate([uneven, jnp.where(lane == nc - 1, 0.0, pltpu.roll(even, nc - 1, axis=1))], axis=1)
        w, u, v = [fine[f, lf, rp] for f in range(3)]
        flux = advect(w, centre, lower, upper) + advect(v, centre, before, after) + advect(u, centre, left, right)
        around = (lower + upper) + (before + after) + (left + right)
        return centre, (4.0 * salt_diffusion) * (around - 6.0 * centre) - 2.0 * flux

    mean_mid = []
    for l in range(2):
        total = None
        for lf in (2 * l, 2 * l + 1):
            for rp in range(2):
                centre, rate = salt_rate(grains, lf, rp)
                mid = centre + time_step * rate
                grains_mid[lf + 1, rp, OFF : OFF + nr] = mid
                total = mid if total is None else total + mid
        mean_mid.append(0.125 * halves(total))
    walls(grains_mid)
    rim_start(grains_mid, 1)

    mean_landed(0).wait_recv()

    @pl.when(r > 0)
    def _():
        mean_landed(1).wait_recv()
        mean_landed(2).wait_recv()

    @pl.when(r < last)
    def _():
        mean_landed(3).wait_recv()
        mean_landed(4).wait_recv()

    for l in range(4):
        heat_part = warm_mean(0, l, frame)
        buoy[l] = heat_part - contraction * mean_salt[l, lo : lo + frame]

    def coarse_step(buf, level, start, count, lift):
        here = lax.broadcasted_iota(jnp.int32, (count, nc), 1)
        rows = pl.ds(start, count)
        centres = [buf[f, level, rows] for f in range(4)]
        out = []
        for f in range(4):
            q = centres[f]
            lower, upper = buf[f, level - 1, rows], buf[f, level + 1, rows]
            before, after = buf[f, level, start - 1 : start - 1 + count], buf[f, level, start + 1 : start + 1 + count]
            left = jnp.where(here == 0, 0.0, pltpu.roll(q, 1, axis=1))
            right = jnp.where(here == nc - 1, 0.0, pltpu.roll(q, nc - 1, axis=1))
            flux = (
                advect(centres[0], q, lower, upper)
                + advect(centres[1], q, left, right)
                + advect(centres[2], q, before, after)
            )
            around = (lower + upper) + (before + after) + (left + right)
            rate = diffusion[f] * (around - 6.0 * q) - flux
            out.append((q, rate + lift if f == 0 else rate))
        return out

    row = lax.broadcasted_iota(jnp.int32, (frame, nc), 0) + (r * nr - WIDE)
    inside = jnp.logical_and(row >= 0, row < (last + 1) * nr)
    for f in range(4):
        for level in range(4):
            mids[f, level + 1, 0:8] = jnp.zeros((8, nc), f32)
            mids[f, level + 1, OFF + nr : padded] = jnp.zeros((8, nc), f32)
    for level in range(4):
        for f, (q, rate) in enumerate(coarse_step(fields, level + 1, lo, frame, buoy[level])):
            mids[f, level + 1, lo : lo + frame] = jnp.where(inside, q + time_step * rate, 0.0)

    for z in range(2):
        refine_rows(mids, z, OFF, nr)
    results = []
    for l in range(2):
        lift = warm_mean(2 * gz, l, nr) - contraction * mean_mid[l]
        level = gz * 2 + l + 1
        steps = coarse_step(mids, level, OFF, nr, lift)
        results.append(
            [0.5 * fields[f, level, OFF : OFF + nr] + 0.5 * (q + time_step * rate) for f, (q, rate) in enumerate(steps)]
        )
    for a in range(n // per):
        for t in range(lanes // 128):
            values = []
            for k in range(per):
                pair = per * t + k
                values.append(results[pair % 2][pair // 2][:, 128 * a : 128 * (a + 1)])
            for j in range(per):
                outgoing[per * a + j, :, 128 * t : 128 * (t + 1)] = gather_chunks(values, j)
    ends = []
    for d in range(1, n):
        to = lax.rem(gy + d, n)
        ends.append(remote(outgoing.at[to], landed.at[gy], end_send.at[d], end_recv.at[gy], gx, to, gz))
        ends[-1].start()
    landed[gy] = outgoing[gy]

    refine_speeds()
    rim_wait(grains_mid, 1)
    parts = []
    for lf in range(4):
        for rp in range(2):
            centre, rate = salt_rate(grains_mid, lf, rp)
            parts.append(0.5 * grains[lf + 1, rp, OFF : OFF + nr] + 0.5 * (centre + time_step * rate))
    whole = split_dot(jnp.concatenate(parts, axis=0), fold[...], ((1,), (1,)))
    for lf in range(4):
        for rp in range(2):
            k = (lf * 2 + rp) * nr
            for c in range(nc // 64):
                salt[lf, c, pl.ds(rp, nr, stride=2), :] = whole[k : k + nr, 128 * c : 128 * (c + 1)]

    stores = [
        pltpu.make_async_copy(salt.at[:, c], salt_out.at[:, :, 128 * c : 128 * (c + 1)], load.at[2 + c])
        for c in range(nc // 64)
    ]
    for copy in stores:
        copy.start()

    for d in range(1, n):
        j = lax.rem(gy + n - d, n)
        remote(outgoing.at[j], landed.at[j], end_send.at[d], end_recv.at[j], gx, j, gz).wait_recv()
    back = landed[...].reshape(ny, lanes).T
    flow[...] = back[: 6 * cx].reshape(3, 2, cx, ny)
    heat[...] = back[6 * cx :].reshape(2, cx, ny)
    stores += [pltpu.make_async_copy(flow, vel_out, load.at[0]), pltpu.make_async_copy(heat, heat_out, load.at[1])]
    for copy in stores[-2:]:
        copy.start()

    for copy in main + ends:
        copy.wait_send()
    for j in range(n):
        passed(j, gz).wait_send()
    mean_copy(0).wait_send()

    @pl.when(gx < ngx - 1)
    def _():
        for z in range(2):
            edge_copy(0, z).wait_send()

    @pl.when(gx > 0)
    def _():
        for z in range(2):
            edge_copy(1, z).wait_send()

    @pl.when(r < last)
    def _():
        mean_copy(1).wait_send()
        mean_copy(2).wait_send()

    @pl.when(r > 0)
    def _():
        mean_copy(3).wait_send()
        mean_copy(4).wait_send()

    for copy in stores:
        copy.wait()


def store(*refs):
    ins, outs, held, sems = refs[:3], refs[3:6], refs[6:9], refs[9]
    pairs = []
    for k in range(3):
        for i in range(ins[k].shape[0]):
            sem = sems.at[k, i]
            pairs.append(
                (
                    pltpu.make_async_copy(ins[k].at[i], held[k].at[i], sem),
                    pltpu.make_async_copy(held[k].at[i], outs[k].at[i], sem),
                )
            )
    for first, _ in pairs:
        first.start()
    for first, second in pairs:
        first.wait()
        second.start()
    for _, second in pairs:
        second.wait()


def on_device(ngx, n, flow, heat, salt):
    cx, ny = flow.shape[2], flow.shape[3]
    nr, nc = salt.shape[1] // 2, salt.shape[2] // 2
    padded = nr + 2 * OFF
    lanes = 8 * cx
    f32, dma = jnp.float32, pltpu.SemaphoreType.DMA
    hbm = pl.BlockSpec(memory_space=pltpu.HBM)
    vel, temp, out = pl.pallas_call(
        functools.partial(kernel, ngx, n, nr, nc, cx, ny),
        out_shape=(
            jax.ShapeDtypeStruct(flow.shape, f32),
            jax.ShapeDtypeStruct(heat.shape, f32),
            jax.ShapeDtypeStruct(salt.shape, f32),
        ),
        in_specs=[hbm] * 3,
        out_specs=(hbm,) * 3,
        scratch_shapes=[
            pltpu.VMEM(flow.shape, f32),
            pltpu.VMEM(heat.shape, f32),
            pltpu.VMEM((4, nc // 64, 2 * nr, 128), f32),
            pltpu.VMEM((ny + 16, lanes), f32),
            pltpu.VMEM((n, nr + 8, lanes), f32),
            pltpu.VMEM((2, 8, lanes), f32),
            pltpu.VMEM((2, n, nr + 8, lanes), f32),
            pltpu.VMEM((2, n, 8, lanes), f32),
            pltpu.VMEM((4, 6, padded, nc), f32),
            pltpu.VMEM((4, 6, padded, nc), f32),
            pltpu.VMEM((4, 8, 2, nr + 2 * WIDE, nc), f32),
            pltpu.VMEM((3, 4, 2, nr, 2 * nc), f32),
            pltpu.VMEM((6, 2, padded, 2 * nc), f32),
            pltpu.VMEM((6, 2, padded, 2 * nc), f32),
            pltpu.VMEM((4, padded, nc), f32),
            pltpu.VMEM((4, nr + 2 * WIDE, nc), f32),
            pltpu.VMEM((n, nr, lanes), f32),
            pltpu.VMEM((n, nr, lanes), f32),
            pltpu.VMEM((2 * nc, 2 * nc), jnp.bfloat16),
            pltpu.VMEM((nc, 2 * nc), jnp.bfloat16),
            dma((n,)), dma((2, n)), dma((n,)), dma((2, 2)), dma((2, n)), dma((5,)), dma((5,)),
            dma((2, 3)), dma((2, 3)), dma((n,)), dma((n,)), dma((2 + nc // 64,)),
        ],
        compiler_params=pltpu.CompilerParams(
            collective_id=0, has_side_effects=True, vmem_limit_bytes=VMEM
        ),
    )(flow, heat, salt)
    return pl.pallas_call(
        store,
        out_shape=tuple(jax.ShapeDtypeStruct(a.shape, f32) for a in (flow, heat, salt)),
        in_specs=[hbm] * 3,
        out_specs=(hbm,) * 3,
        scratch_shapes=[pltpu.VMEM(a.shape, f32) for a in (flow, heat, salt)] + [dma((3, 4))],
        compiler_params=pltpu.CompilerParams(vmem_limit_bytes=VMEM),
    )(vel, temp, out)


def solution(mesh):
    in_specs = (P(None, "gz", "gy", "gx"), P("gz", "gy", "gx"), P("gz", ("gx", "gy"), None))
    out_specs = (P(None, "gz", "gy", "gx"), P("gz", "gy", "gx"), P("gz", ("gx", "gy"), None))
    return jax.shard_map(
        functools.partial(on_device, mesh.shape["gx"], mesh.shape["gy"]),
        mesh=mesh, in_specs=in_specs, out_specs=out_specs, check_vma=False,
    )
```
